128 devices in a mesh: dev: 128 (over y, z, x, core).
Axes of the slice: x: 4, y: 4, z: 4, core: 2. Of those that a mesh axis runs over, the one named last changes fastest.
Arguments:
- density_rows: bfloat16 [98304, 3840], P('dev')
- center_x: float32 [98304], replicated, may hold values from -0.25 to 1.25
- center_y: float32 [98304], replicated, may hold values from 0 to 1
- center_z: float32 [98304], replicated, may hold values from 0 to 1
- exponent: float32 [98304], replicated, may hold values from 0.5 to 150
- brick_blocks: int32 [128, 8], replicated, may hold values from 0 to 767, as said below
Outputs:
- potential: float32 [128, 4096], P('dev')
- ham_rows: float32 [98304, 3840], P('dev')
The draws below stay inside these ranges and needn't reach their ends.
Inputs may be any that keep to these rules, and one draw needn't show every extreme that they name: `brick_blocks`: brick b belongs to device d = b. Its 8 entries are distinct blocks; 4 of them are owned by one of the devices d - 1, d, d + 1 (cyclically) and 2 by each of the other two, where block I is owned by device I // 6. Which of the three owns 4 changes from brick to brick. Blocks 0 and 767 touch brick 0.
All inputs are finite; a program needn't handle non-finite values.
Results may differ from the reference program's by a relative error of at most 0.00041.
Values may be sent and summed in bfloat16 or wider, within the bound.
No kernel may reach another device: no remote copies, remote signals or barrier semaphores. Data moves between devices by JAX's collectives and lax.ppermute only.
A program may use at most 128 MiB of HBM per device.

```python
import math
import jax
import jax.numpy as jnp
from jax import lax

FB = 128
KB = 8
CAP = 4
BLK_DEV = 6
SIDE = 16
BR_DEV = 1
NF = 98304
N_DEV = 128


def draw_density_rows(key, part):
    row_count = N_DEV * BLK_DEV * FB
    col_count = 5 * BLK_DEV * FB
    row_index = jnp.arange(row_count, dtype=jnp.int32)[:, None]
    col_index = jnp.arange(col_count, dtype=jnp.int32)[None, :]
    owner_dev = (row_index // (BLK_DEV * FB)).astype(jnp.float32)
    growth = 1.0 + 2.0 * owner_dev / (N_DEV - 1)
    on_diagonal = col_index == 2 * BLK_DEV * FB + row_index % (BLK_DEV * FB)
    random_part = jnp.clip(jax.random.normal(key, (row_count, col_count), jnp.float32), -6.0, 6.0)
    values = (0.2 * random_part + 2.0 * growth * on_diagonal.astype(jnp.float32)) / (KB * FB)
    return values.astype(jnp.bfloat16)


def draw_brick_blocks(key, part):
    base_key = jax.random.fold_in(key, 11)

    def one_brick(brick):
        brick_key = jax.random.fold_in(base_key, brick)
        device = brick // BR_DEV
        heavy_side = jax.random.randint(jax.random.fold_in(brick_key, 7), (), 0, 3)
        counts = jnp.where(jnp.arange(3) == heavy_side, CAP, (KB - CAP) // 2)
        owners = jnp.mod(device + jnp.arange(3) - 1, N_DEV)
        shuffled_list = []
        for side in range(3):
            perm = jax.random.permutation(jax.random.fold_in(brick_key, side), BLK_DEV).astype(jnp.int32)
            target = jnp.where(owners[side] == 0, 0, jnp.where(owners[side] == N_DEV - 1, BLK_DEV - 1, -1))
            found = (perm == target).astype(jnp.int32)
            position = jnp.sum(found * jnp.arange(BLK_DEV, dtype=jnp.int32))
            rolled = perm[jnp.mod(jnp.arange(BLK_DEV, dtype=jnp.int32) + position, BLK_DEV)]
            use_roll = (brick == 0) & (target >= 0)
            shuffled_list.append(jnp.where(use_roll, rolled, perm))
        shuffled = jnp.stack(shuffled_list)
        chosen = jnp.arange(BLK_DEV)[None, :] < counts[:, None]
        ordering = jnp.argsort(jnp.where(chosen, 0, 1).reshape(-1), stable=True)[:KB]
        blocks = (owners[:, None] * BLK_DEV + shuffled).reshape(-1)
        return blocks[ordering].astype(jnp.int32)
    return lax.map(one_brick, jnp.arange(N_DEV * BR_DEV, dtype=jnp.int32))


def setup_inputs(seed: int = 0) -> dict:
    key_of = jax.random.split(jax.random.key(seed), 7)
    return {
        "density_rows": draw_density_rows(jax.random.fold_in(key_of[6], 71), 0),
        "center_x": jnp.clip(jax.random.uniform(key_of[1], (NF,), jnp.float32, -0.25, 1.25), -0.25, 1.25),
        "center_y": jnp.clip(jax.random.uniform(key_of[2], (NF,), jnp.float32, 0.0, 1.0), 0.0, 1.0),
        "center_z": jnp.clip(jax.random.uniform(key_of[3], (NF,), jnp.float32, 0.0, 1.0), 0.0, 1.0),
        "exponent": jnp.clip(jnp.exp(jax.random.uniform(key_of[4], (NF,), jnp.float32, math.log(0.5), math.log(150.0))), 0.5, 150.0),
        "brick_blocks": draw_brick_blocks(jax.random.fold_in(key_of[6], 71), 0),
    }


omega = 2.0 / 3.0
four_pi = 4.0 * math.pi
slater = (3.0 / math.pi) ** (1.0 / 3.0)


def periodic(distance, period):
    return jnp.mod(distance + 0.5 * period, period) - 0.5 * period


def basis_values(device, z_slot, blocks, center_x, center_y, center_z, exponent, devices):
    functions = (blocks[:, None] * FB + jnp.arange(FB, dtype=jnp.int32)[None, :]).reshape(-1)
    owner_dev = functions // (BLK_DEV * FB)
    offset = (jnp.mod(device - owner_dev + 1, devices) - 1).astype(jnp.float32)
    grid_points = (jnp.arange(SIDE, dtype=jnp.float32) + 0.5) / SIDE
    decay_rate = exponent[functions][:, None]
    along_x = offset[:, None] + grid_points[None, :] - center_x[functions][:, None]
    along_y = periodic(grid_points[None, :] - center_y[functions][:, None], 1.0)
    along_z = periodic(z_slot + grid_points[None, :] - center_z[functions][:, None], 1.0 * BR_DEV)
    factor_x = jnp.exp(-decay_rate * along_x * along_x)
    factor_y = jnp.exp(-decay_rate * along_y * along_y)
    factor_z = jnp.exp(-decay_rate * along_z * along_z)
    values = factor_x[:, :, None, None] * factor_y[:, None, :, None] * factor_z[:, None, None, :]
    return values.reshape(functions.shape[0], SIDE * SIDE * SIDE).astype(jnp.bfloat16)


def reference(density_rows, center_x, center_y, center_z, exponent, brick_blocks):
    nbricks = N_DEV * BR_DEV
    cells = SIDE * SIDE * SIDE
    density_tiles = density_rows.reshape(N_DEV * BLK_DEV, FB, 5 * BLK_DEV, FB)

    def layout(brick):
        blocks = brick_blocks[brick]
        owner_dev = blocks // BLK_DEV
        col_blocks = jnp.mod(owner_dev[None, :] - owner_dev[:, None] + 2, N_DEV) * BLK_DEV + (blocks % BLK_DEV)[None, :]
        orbitals = basis_values((brick // BR_DEV).astype(jnp.int32), (brick % BR_DEV).astype(jnp.float32), blocks,
                                center_x, center_y, center_z, exponent, N_DEV)
        return blocks, col_blocks, orbitals

    def one_density(brick):
        blocks, col_blocks, orbitals = layout(brick)
        pieces = density_tiles[blocks[:, None], :, col_blocks, :]
        matrix = pieces.transpose(0, 2, 1, 3).reshape(KB * FB, KB * FB)
        applied = jnp.dot(matrix, orbitals, preferred_element_type=jnp.float32)
        return jnp.sum(orbitals.astype(jnp.float32) * applied, axis=0)

    density = lax.map(one_density, jnp.arange(nbricks, dtype=jnp.int32))
    average = jnp.sum(density) / (nbricks * cells)
    source = density - average
    sweep_one = (omega * four_pi / 6.0) * source
    grid_field = sweep_one.reshape(N_DEV, BR_DEV, SIDE, SIDE, SIDE).transpose(0, 2, 3, 1, 4)
    grid_field = grid_field.reshape(N_DEV * SIDE, SIDE, BR_DEV * SIDE)
    beside_all = jnp.roll(grid_field, 1, 0) + jnp.roll(grid_field, -1, 0)
    beside_all = beside_all + jnp.roll(grid_field, 1, 1) + jnp.roll(grid_field, -1, 1)
    beside_all = beside_all + jnp.roll(grid_field, 1, 2) + jnp.roll(grid_field, -1, 2)
    beside_all = beside_all.reshape(N_DEV, SIDE, SIDE, BR_DEV, SIDE).transpose(0, 3, 1, 2, 4).reshape(nbricks, cells)
    sweep_two = sweep_one + omega * ((four_pi * source + beside_all) / 6.0 - sweep_one)
    potential = sweep_two - slater * jnp.cbrt(density)

    def add_brick(ham_tiles, brick):
        blocks, col_blocks, orbitals = layout(brick)
        weighted = (orbitals.astype(jnp.float32) * potential[brick][None, :]).astype(jnp.bfloat16)
        ham_brick = jnp.dot(weighted, orbitals.T, preferred_element_type=jnp.float32) * (64.0 / cells)
        pieces = ham_brick.reshape(KB, FB, KB, FB).transpose(0, 2, 1, 3)
        return ham_tiles.at[blocks[:, None], :, col_blocks, :].add(pieces), None

    start = jnp.zeros((N_DEV * BLK_DEV, FB, 5 * BLK_DEV, FB), jnp.float32)
    ham_tiles, ignored = lax.scan(add_brick, start, jnp.arange(nbricks, dtype=jnp.int32))
    return potential, ham_tiles.reshape(N_DEV * BLK_DEV * FB, 5 * BLK_DEV * FB)
```

```python
import math

import jax
import jax.numpy as jnp
from jax import lax
from jax.experimental import pallas as pl
from jax.experimental.pallas import tpu as pltpu
from jax.sharding import PartitionSpec as P

FB = 128
KB = 8
BLK_DEV = 6
SIDE = 16
CELLS = SIDE * SIDE * SIDE
WIDE = KB * FB
CHUNK = 1024
N_CHUNK = CELLS // CHUNK
PAIR = 2 * FB

omega = 2.0 / 3.0
four_pi = 4.0 * math.pi
slater = (3.0 / math.pi) ** (1.0 / 3.0)

VMEM = pl.BlockSpec(memory_space=pltpu.VMEM)
SMEM = pl.BlockSpec(memory_space=pltpu.SMEM)
ANY = pl.BlockSpec(memory_space=pl.ANY)


def list_blocks(devices, side, bricks_ref, order_ref, count_ref):
    own = lax.axis_index("dev")
    brick = lax.rem(own + side + devices, devices)
    ids = [bricks_ref[brick, k] for k in range(KB)]
    held = [(i // BLK_DEV == own).astype(jnp.int32) for i in ids]
    count = sum(held)
    first, second = jnp.int32(0), count
    for i, h in zip(ids, held):
        at = jnp.where(h == 1, first, second)
        order_ref[(side + 1) * KB + at] = i
        first, second = first + h, second + 1 - h
    count_ref[side + 1] = count


def factors(devices, side, order_ref, cx_ref, cy_ref, cz_ref, ex_ref, x_ref, y_ref, z_ref):
    own = lax.axis_index("dev")
    brick = lax.rem(own + side + devices, devices)
    points = (lax.broadcasted_iota(jnp.int32, (SIDE, FB), 0).astype(jnp.float32) + 0.5) / SIDE
    for k in range(KB):
        block = order_ref[(side + 1) * KB + k]
        offset = (lax.rem(brick - block // BLK_DEV + 1 + devices, devices) - 1).astype(jnp.float32)
        row = pl.ds(block, 1)
        decay = -ex_ref[row, :]
        lanes = pl.ds(k * FB, FB)
        along_x = (offset + points) - cx_ref[row, :]
        x_ref[:, lanes] = jnp.exp(decay * along_x * along_x)
        for c_ref, out_ref in ((cy_ref, y_ref), (cz_ref, z_ref)):
            away = points - c_ref[row, :] + 0.5
            away = away - jnp.floor(away) - 0.5
            out_ref[:, lanes] = jnp.exp(decay * away * away)


def orbital_chunk(chunk, x_ref, y_ref, z_ref, xy_ref, orb_ref):
    layers = CHUNK // (SIDE * SIDE)
    for i in range(layers):
        xy_ref[pl.ds(i * SIDE, SIDE), :] = x_ref[pl.ds(chunk * layers + i, 1), :] * y_ref[...]

    def rows(r, carry):
        for u in range(4):
            ij = r * 4 + u
            values = xy_ref[pl.ds(ij, 1), :] * z_ref[...]
            orb_ref[pl.ds(pl.multiple_of(ij * SIDE, SIDE), SIDE), :] = values.astype(jnp.bfloat16)
        return carry

    lax.fori_loop(0, layers * SIDE // 4, rows, 0)


def density_kernel(
    devices, bricks_ref, cx_ref, cy_ref, cz_ref, ex_ref, rows_ref,
    left_ref, mid_ref, right_ref, charge_ref,
    order_ref, count_ref, dens_ref, x_ref, y_ref, z_ref, xy_ref, orb_ref, part_ref, sems,
):
    own = lax.axis_index("dev")
    outs = (left_ref, mid_ref, right_ref)
    for side in (-1, 0, 1):
        list_blocks(devices, side, bricks_ref, order_ref, count_ref)
        for half in range(2):

            @pl.when(half * 2 < count_ref[side + 1])
            def _():
                def fetch(at, carry):
                    a, c = at // KB, lax.rem(at, KB)
                    row_block = order_ref[(side + 1) * KB + half * 2 + a]
                    col_block = order_ref[(side + 1) * KB + c]
                    row = lax.rem(row_block, BLK_DEV)
                    col = lax.rem(col_block // BLK_DEV - own + 2 + devices, devices) * BLK_DEV + lax.rem(col_block, BLK_DEV)
                    pltpu.make_async_copy(
                        rows_ref.at[pl.ds(pl.multiple_of(row * FB, FB), FB), pl.ds(pl.multiple_of(col * FB, FB), FB)],
                        dens_ref.at[
                            side + 1,
                            half,
                            pl.ds(pl.multiple_of(a * FB, FB), FB),
                            pl.ds(pl.multiple_of(c * FB, FB), FB),
                        ],
                        sems.at[side + 1, half],
                    ).start()
                    return carry

                lax.fori_loop(0, 2 * KB, fetch, 0)

    for side in (-1, 0, 1):
        factors(devices, side, order_ref, cx_ref, cy_ref, cz_ref, ex_ref, x_ref, y_ref, z_ref)
        halves = count_ref[side + 1] // 2
        for half in range(2):

            @pl.when(half < halves)
            def _():
                pltpu.make_async_copy(
                    rows_ref.at[pl.ds(0, PAIR), pl.ds(0, WIDE)], dens_ref.at[side + 1, half], sems.at[side + 1, half]
                ).wait()

        def one_chunk(chunk, carry):
            orbital_chunk(chunk, x_ref, y_ref, z_ref, xy_ref, orb_ref)
            part_ref[...] = jnp.zeros_like(part_ref)

            def one_half(half, inner):
                applied = lax.dot_general(
                    orb_ref[...], dens_ref[side + 1, half], (((1,), (1,)), ((), ())),
                    preferred_element_type=jnp.float32,
                )
                mine = orb_ref[:, pl.ds(pl.multiple_of(half * PAIR, PAIR), PAIR)].astype(jnp.float32)
                product = applied * mine
                part_ref[...] += product[:, :FB] + product[:, FB:]
                return inner

            lax.fori_loop(0, halves, one_half, 0)
            summed = jnp.sum(part_ref[...].T, axis=0, keepdims=True)
            outs[side + 1][:, pl.ds(pl.multiple_of(chunk * CHUNK, CHUNK), CHUNK)] = summed
            return carry

        lax.fori_loop(0, N_CHUNK, one_chunk, 0)
    total = left_ref[...] + mid_ref[...] + right_ref[...]
    charge = total[:, :FB]
    for k in range(1, CELLS // FB):
        charge = charge + total[:, k * FB : (k + 1) * FB]
    charge_ref[...] = charge


def add_kernel(a_ref, b_ref, c_ref, dens_ref, head_ref, tail_ref):
    dens = a_ref[...] + b_ref[...] + c_ref[...]
    dens_ref[...] = dens
    head_ref[...] = dens[:, : SIDE * SIDE]
    tail_ref[...] = dens[:, CELLS - SIDE * SIDE :]


def potential_of(density, before, after, average):
    layer = SIDE * SIDE
    lane = lax.broadcasted_iota(jnp.int32, density.shape, 1)
    along_z = lane & (SIDE - 1)
    along_y = (lane // SIDE) & (SIDE - 1)
    scale = omega * four_pi / 6.0
    source = density - average
    one = scale * source
    padded = jnp.concatenate([scale * (before - average), one, scale * (after - average)], axis=1)
    beside = padded[:, : CELLS] + padded[:, 2 * layer :]

    def moved(steps):
        return pltpu.roll(one, steps % CELLS, 1)

    beside += jnp.where(along_y > 0, moved(SIDE), moved(SIDE - layer))
    beside += jnp.where(along_y < SIDE - 1, moved(-SIDE), moved(layer - SIDE))
    beside += jnp.where(along_z > 0, moved(1), moved(1 - SIDE))
    beside += jnp.where(along_z < SIDE - 1, moved(-1), moved(SIDE - 1))
    two = one + omega * ((four_pi * source + beside) / 6.0 - one)
    root = jnp.exp(jnp.log(jnp.abs(density)) * (1.0 / 3.0))
    return two - slater * jnp.where(density < 0.0, -root, root)


def ham_kernel(
    devices, bricks_ref, cx_ref, cy_ref, cz_ref, ex_ref,
    left_ref, mid_ref, right_ref, before_ref, after_ref, charge_ref,
    pot_ref, ham_ref,
    order_ref, count_ref, v_ref, x_ref, y_ref, z_ref, xy_ref, orb_ref, acc_ref,
):
    own = lax.axis_index("dev")
    layer = SIDE * SIDE

    def wide(ref):
        return jnp.broadcast_to(ref[...], (8, ref.shape[1]))

    average = jnp.sum(charge_ref[...]) / (devices * CELLS)
    left, mid, right = wide(left_ref), wide(mid_ref), wide(right_ref)
    v_ref[0] = potential_of(left, wide(before_ref), mid[:, :layer], average)
    own_potential = potential_of(mid, left[:, CELLS - layer :], right[:, :layer], average)
    v_ref[1] = own_potential
    v_ref[2] = potential_of(right, mid[:, CELLS - layer :], wide(after_ref), average)
    pot_ref[...] = own_potential[:1]
    ham_ref[...] = jnp.zeros_like(ham_ref)
    for side in (-1, 0, 1):
        list_blocks(devices, side, bricks_ref, order_ref, count_ref)
        factors(devices, side, order_ref, cx_ref, cy_ref, cz_ref, ex_ref, x_ref, y_ref, z_ref)
        halves = count_ref[side + 1] // 2
        acc_ref[...] = jnp.zeros_like(acc_ref)

        def one_chunk(chunk, carry):
            orbital_chunk(chunk, x_ref, y_ref, z_ref, xy_ref, orb_ref)
            v = v_ref[side + 1, pl.ds(0, 1), pl.ds(pl.multiple_of(chunk * CHUNK, CHUNK), CHUNK)]

            def one_half(half, inner):
                mine = orb_ref[:, pl.ds(pl.multiple_of(half * PAIR, PAIR), PAIR)].T
                weighted = (mine.astype(jnp.float32) * v).astype(jnp.bfloat16)
                acc_ref[half] += jnp.dot(weighted, orb_ref[...], preferred_element_type=jnp.float32)
                return inner

            lax.fori_loop(0, halves, one_half, 0)
            return carry

        lax.fori_loop(0, N_CHUNK, one_chunk, 0)

        def put(at, carry):
            half, rest = at // (2 * KB), lax.rem(at, 2 * KB)
            a, c = rest // KB, lax.rem(rest, KB)
            row_block = order_ref[(side + 1) * KB + half * 2 + a]
            col_block = order_ref[(side + 1) * KB + c]
            row = lax.rem(row_block, BLK_DEV)
            col = lax.rem(col_block // BLK_DEV - own + 2 + devices, devices) * BLK_DEV + lax.rem(col_block, BLK_DEV)
            piece = acc_ref[half, pl.ds(pl.multiple_of(a * FB, FB), FB), pl.ds(pl.multiple_of(c * FB, FB), FB)]
            ham_ref[
                pl.ds(pl.multiple_of(row * FB, FB), FB), pl.ds(pl.multiple_of(col * FB, FB), FB)
            ] += piece * (64.0 / CELLS)
            return carry

        lax.fori_loop(0, halves * 2 * KB, put, 0)


def f32(*shape):
    return jax.ShapeDtypeStruct(shape, jnp.float32)


def moved_by(value, steps, devices):
    return lax.ppermute(value, "dev", [(i, (i + steps) % devices) for i in range(devices)])


def solution(mesh):
    devices = mesh.shape["dev"]

    def shared_scratch():
        return [
            pltpu.VMEM((SIDE, WIDE), jnp.float32),
            pltpu.VMEM((SIDE, WIDE), jnp.float32),
            pltpu.VMEM((SIDE, WIDE), jnp.float32),
            pltpu.VMEM((CHUNK // SIDE, WIDE), jnp.float32),
            pltpu.VMEM((CHUNK, WIDE), jnp.bfloat16),
        ]

    def lists():
        return [pltpu.SMEM((3 * KB,), jnp.int32), pltpu.SMEM((3,), jnp.int32)]

    def local(density_rows, center_x, center_y, center_z, exponent, brick_blocks):
        tables = [t.reshape(-1, FB) for t in (center_x, center_y, center_z, exponent)]
        to_left, kept, to_right, charge = pl.pallas_call(
            lambda *refs: density_kernel(devices, *refs),
            out_shape=[f32(1, CELLS), f32(1, CELLS), f32(1, CELLS), f32(1, FB)],
            in_specs=[SMEM] + [VMEM] * 4 + [ANY],
            out_specs=[VMEM] * 4,
            scratch_shapes=lists()
            + [pltpu.VMEM((3, 2, PAIR, WIDE), jnp.bfloat16)]
            + shared_scratch()
            + [pltpu.VMEM((CHUNK, FB), jnp.float32), pltpu.SemaphoreType.DMA((3, 2))],
            compiler_params=pltpu.CompilerParams(vmem_limit_bytes=48 * 2**20),
        )(brick_blocks, *tables, density_rows)
        from_right = moved_by(to_left, -1, devices)
        from_left = moved_by(to_right, 1, devices)
        steps = 1
        while steps < devices:
            charge = charge + lax.ppermute(charge, "dev", [(i, i ^ steps) for i in range(devices)])
            steps *= 2
        density, head, tail = pl.pallas_call(
            add_kernel,
            out_shape=[f32(1, CELLS), f32(1, SIDE * SIDE), f32(1, SIDE * SIDE)],
            in_specs=[VMEM] * 3,
            out_specs=[VMEM] * 3,
        )(kept, from_left, from_right)
        left = moved_by(density, 1, devices)
        right = moved_by(density, -1, devices)
        before = moved_by(tail, 2, devices)
        after = moved_by(head, -2, devices)
        return pl.pallas_call(
            lambda *refs: ham_kernel(devices, *refs),
            out_shape=[f32(1, CELLS), f32(BLK_DEV * FB, 5 * BLK_DEV * FB)],
            in_specs=[SMEM] + [VMEM] * 10,
            out_specs=[VMEM] * 2,
            scratch_shapes=lists()
            + [pltpu.VMEM((3, 8, CELLS), jnp.float32)]
            + shared_scratch()
            + [pltpu.VMEM((2, PAIR, WIDE), jnp.float32)],
            compiler_params=pltpu.CompilerParams(vmem_limit_bytes=48 * 2**20),
        )(brick_blocks, *tables, left, density, right, before, after, charge)

    def program(density_rows, center_x, center_y, center_z, exponent, brick_blocks):
        potential, ham = local(density_rows, center_x, center_y, center_z, exponent, brick_blocks)
        return potential, ham

    return jax.shard_map(
        program,
        mesh=mesh,
        in_specs=(P("dev", None), P(), P(), P(), P(), P()),
        out_specs=(P("dev", None), P("dev", None)),
        check_vma=False,
    )
```

```python
import math

import jax
import jax.numpy as jnp
from jax import lax
from jax.experimental import pallas as pl
from jax.experimental.pallas import tpu as pltpu
from jax.sharding import PartitionSpec as P

FB = 128
KB = 8
BLK_DEV = 6
SIDE = 16
LAYER = SIDE * SIDE
CELLS = SIDE * LAYER
WIDE = KB * FB
CHUNK = 1024
SUB = 256
PAIR = 2 * FB
TILE = 8
TILES = 5
COLS = 5 * BLK_DEV

omega = 2.0 / 3.0
four_pi = 4.0 * math.pi
slater = (3.0 / math.pi) ** (1.0 / 3.0)

VMEM = pl.BlockSpec(memory_space=pltpu.VMEM)
SMEM = pl.BlockSpec(memory_space=pltpu.SMEM)
HBM = pl.BlockSpec(memory_space=pltpu.HBM)
LIMIT = 48 * 2**20


def aligned(index, unit):
    return pl.ds(pl.multiple_of(index * unit, unit), unit)


def wrap(value, count):
    return lax.rem(value + 2 * count, count)


def list_blocks(devices, bricks_ref, order_ref, count_ref):
    own = lax.axis_index("dev")
    for side in range(3):
        brick = wrap(own + side - 1, devices)
        ids = [bricks_ref[k, brick] for k in range(KB)]
        held = [(i // BLK_DEV == own).astype(jnp.int32) for i in ids]
        first, second = jnp.int32(0), sum(held)
        count_ref[side] = second
        for i, h in zip(ids, held):
            order_ref[side * KB + jnp.where(h == 1, first, second)] = i
            first, second = first + h, second + 1 - h


def place(devices, order_ref, side, a, c):
    own = lax.axis_index("dev")
    row_block, col_block = order_ref[side * KB + a], order_ref[side * KB + c]
    col = wrap(col_block // BLK_DEV - own + 2, devices) * BLK_DEV + lax.rem(col_block, BLK_DEV)
    return lax.rem(row_block, BLK_DEV), col


def first_tile(devices):
    own = lax.axis_index("dev")
    return wrap((own - 2) * BLK_DEV, devices * BLK_DEV) // TILE


def fetch_tables(devices, table_refs, tables_ref, sem):
    base = first_tile(devices)
    for t, table_ref in enumerate(table_refs):
        for k in range(TILES):
            tile = lax.rem(base + k, devices * BLK_DEV // TILE)
            pltpu.make_async_copy(
                table_ref.at[aligned(tile, TILE), :], tables_ref.at[t, pl.ds(k * TILE, TILE), :], sem
            ).start()


def factors(devices, side, order_ref, tables_ref, x_ref, y_ref, z_ref):
    own = lax.axis_index("dev")
    brick = wrap(own + side - 1, devices)
    base = first_tile(devices) * TILE
    points = (lax.broadcasted_iota(jnp.int32, (SIDE, FB), 0).astype(jnp.float32) + 0.5) / SIDE
    for k in range(KB):
        block = order_ref[side * KB + k]
        offset = (wrap(brick - block // BLK_DEV + 1, devices) - 1).astype(jnp.float32)
        row = pl.ds(wrap(block - base, devices * BLK_DEV), 1)
        decay = -tables_ref[3, row, :]
        lanes = pl.ds(k * FB, FB)
        along_x = (offset + points) - tables_ref[0, row, :]
        x_ref[:, lanes] = jnp.exp(decay * along_x * along_x)
        for t, out_ref in ((1, y_ref), (2, z_ref)):
            away = points - tables_ref[t, row, :] + 0.5
            away = away - jnp.floor(away) - 0.5
            out_ref[:, lanes] = jnp.exp(decay * away * away)


def orbital_chunk(part, step, x_ref, y_ref, z_ref, orb_ref):
    layers = CHUNK // LAYER
    for k in range(KB):
        lanes = slice(k * FB, (k + 1) * FB)
        x = x_ref[aligned(step, 8), lanes]
        y, z = y_ref[:, lanes], z_ref[:, lanes]
        for i in range(layers):
            xy = x[part * layers + i : part * layers + i + 1] * y
            for j in range(SIDE):
                at = (i * SIDE + j) * SIDE
                orb_ref[at : at + SIDE, lanes] = (xy[j : j + 1] * z).astype(jnp.bfloat16)


def density_kernel(
    devices, bricks_ref, cx_ref, cy_ref, cz_ref, ex_ref, rows_ref,
    left_ref, mid_ref, right_ref, zero_out_ref,
    order_ref, count_ref, tables_ref, x_ref, y_ref, z_ref, orb_a, orb_b, dens_ref, zero_ref, res_ref,
    table_sem, dens_sems, zero_sems,
):
    fetch_tables(devices, (cx_ref, cy_ref, cz_ref, ex_ref), tables_ref, table_sem)
    list_blocks(devices, bricks_ref, order_ref, count_ref)

    def fetch_brick(side, carry):
        def fetch(at, inner):
            a, c = at // KB, lax.rem(at, KB)
            row, col = place(devices, order_ref, side, a, c)
            pltpu.make_async_copy(
                rows_ref.at[aligned(row, FB), aligned(col, FB)],
                dens_ref.at[side, aligned(a, FB), aligned(c, FB)],
                dens_sems.at[side, a // 2],
            ).start()
            return inner

        return lax.fori_loop(0, count_ref[side] * KB, fetch, carry)

    lax.fori_loop(0, 3, fetch_brick, 0)
    zero_ref[...] = jnp.zeros_like(zero_ref)
    zero_copies = [
        pltpu.make_async_copy(zero_ref, zero_out_ref.at[pl.ds(r * FB, FB), :], zero_sems.at[r]) for r in range(BLK_DEV)
    ]
    for copy in zero_copies:
        copy.start()
    pltpu.make_async_copy(tables_ref, tables_ref, table_sem).wait()

    def one_brick(side, carry):
        factors(devices, side, order_ref, tables_ref, x_ref, y_ref, z_ref)

        def await_half(half, inner):
            pltpu.make_async_copy(
                rows_ref.at[pl.ds(0, PAIR), pl.ds(0, WIDE)],
                dens_ref.at[side, aligned(half, PAIR), :],
                dens_sems.at[side, half],
            ).wait()
            return inner

        lax.fori_loop(0, count_ref[side] // 2, await_half, 0)

        def steps(rows):
            def step(t, inner):
                for part, orb_ref in ((0, orb_a), (1, orb_b)):
                    orbital_chunk(part, t, x_ref, y_ref, z_ref, orb_ref)
                    for s in range(0, CHUNK, SUB):
                        applied = lax.dot_general(
                            orb_ref[s : s + SUB, :], dens_ref[side, :rows, :], (((1,), (1,)), ((), ())),
                            preferred_element_type=jnp.float32,
                        )
                        product = applied * orb_ref[s : s + SUB, :rows].astype(jnp.float32)
                        total = product[:, :FB]
                        for k in range(FB, rows, FB):
                            total = total + product[:, k : k + FB]
                        at = pl.ds(pl.multiple_of(t * 2 * CHUNK + part * CHUNK + s, SUB), SUB)
                        res_ref[side, :, at] = jnp.sum(total.T, axis=0, keepdims=True)
                return inner

            lax.fori_loop(0, CELLS // (2 * CHUNK), step, 0)

        pl.when(count_ref[side] == 2)(lambda: steps(PAIR))
        pl.when(count_ref[side] != 2)(lambda: steps(2 * PAIR))
        return carry

    lax.fori_loop(0, 3, one_brick, 0)
    total = res_ref[0] + res_ref[1] + res_ref[2]
    charge = total[:, :FB]
    for k in range(1, CELLS // FB):
        charge = charge + total[:, k * FB : (k + 1) * FB]
    for side, ref in enumerate((left_ref, mid_ref, right_ref)):
        ref[:, :CELLS] = res_ref[side]
        ref[:, CELLS:] = charge
    for copy in zero_copies:
        copy.wait()


def add_kernel(kept_ref, left_ref, right_ref, dens_ref, head_ref, tail_ref):
    dens = kept_ref[:, :CELLS] + left_ref[:, :CELLS] + right_ref[:, :CELLS]
    dens_ref[...] = dens
    head_ref[...] = dens[:, :LAYER]
    tail_ref[:, :LAYER] = dens[:, CELLS - LAYER :]
    tail_ref[:, LAYER:] = kept_ref[:, CELLS:] + left_ref[:, CELLS:]


def potential_of(density, before, after, average):
    lane = lax.broadcasted_iota(jnp.int32, density.shape, 1)
    along_z = lane & (SIDE - 1)
    along_y = (lane // SIDE) & (SIDE - 1)
    scale = omega * four_pi / 6.0
    source = density - average
    one = scale * source
    padded = jnp.concatenate([scale * (before - average), one, scale * (after - average)], axis=1)
    beside = padded[:, :CELLS] + padded[:, 2 * LAYER :]

    def moved(steps):
        return pltpu.roll(one, steps % CELLS, 1)

    beside += jnp.where(along_y > 0, moved(SIDE), moved(SIDE - LAYER))
    beside += jnp.where(along_y < SIDE - 1, moved(-SIDE), moved(LAYER - SIDE))
    beside += jnp.where(along_z > 0, moved(1), moved(1 - SIDE))
    beside += jnp.where(along_z < SIDE - 1, moved(-1), moved(SIDE - 1))
    two = one + omega * ((four_pi * source + beside) / 6.0 - one)
    root = jnp.exp(jnp.log(jnp.abs(density)) * (1.0 / 3.0))
    return two - slater * jnp.where(density < 0.0, -root, root)


def ham_kernel(
    devices, bricks_ref, cx_ref, cy_ref, cz_ref, ex_ref,
    left_ref, mid_ref, right_ref, before_ref, after_ref, charge_ref, zeroed_ref,
    pot_ref, ham_ref,
    order_ref, count_ref, tables_ref, x_ref, y_ref, z_ref, orb_a, orb_b, v_ref, acc_ref, sum_ref, seen_ref,
    table_sem, ham_sems,
):
    fetch_tables(devices, (cx_ref, cy_ref, cz_ref, ex_ref), tables_ref, table_sem)
    list_blocks(devices, bricks_ref, order_ref, count_ref)

    def clear(at, carry):
        seen_ref[at] = 0
        return carry

    lax.fori_loop(0, BLK_DEV * COLS, clear, 0)

    def wide(ref):
        return jnp.broadcast_to(ref[:, :CELLS], (8, min(ref.shape[1], CELLS)))

    average = jnp.sum(charge_ref[...]) / (devices * CELLS)
    left, mid, right = wide(left_ref), wide(mid_ref), wide(right_ref)
    v_ref[0] = potential_of(left, wide(before_ref)[:, :LAYER], mid[:, :LAYER], average)
    own_potential = potential_of(mid, left[:, CELLS - LAYER :], right[:, :LAYER], average)
    v_ref[1] = own_potential
    v_ref[2] = potential_of(right, mid[:, CELLS - LAYER :], wide(after_ref)[:, :LAYER], average)
    pot_ref[...] = own_potential[:1]
    pltpu.make_async_copy(tables_ref, tables_ref, table_sem).wait()

    def await_rows(side, rows_half):
        pltpu.make_async_copy(
            sum_ref.at[pl.ds(0, PAIR), pl.ds(0, WIDE)], ham_ref.at[pl.ds(0, PAIR), pl.ds(0, WIDE)],
            ham_sems.at[side, rows_half],
        ).wait()

    def await_brick(side):
        lax.fori_loop(0, count_ref[side] // 2, lambda half, inner: (await_rows(side, half), inner)[1], 0)

    def one_brick(side, carry):
        factors(devices, side, order_ref, tables_ref, x_ref, y_ref, z_ref)

        def steps(rows):
            def step(t, inner):
                for part, orb_ref in ((0, orb_a), (1, orb_b)):
                    orbital_chunk(part, t, x_ref, y_ref, z_ref, orb_ref)
                    at = pl.ds(pl.multiple_of(t * 2 * CHUNK + part * CHUNK, CHUNK), CHUNK)
                    v = v_ref[side, pl.ds(0, 1), at]
                    mine = orb_ref[:, :rows].T
                    weighted = (mine.astype(jnp.float32) * v).astype(jnp.bfloat16)
                    acc_ref[:rows, :] += jnp.dot(weighted, orb_ref[...], preferred_element_type=jnp.float32)
                return inner

            acc_ref[:rows, :] = jnp.zeros((rows, WIDE), jnp.float32)
            lax.fori_loop(0, CELLS // (2 * CHUNK), step, 0)

        pl.when(count_ref[side] == 2)(lambda: steps(PAIR))
        pl.when(count_ref[side] != 2)(lambda: steps(2 * PAIR))
        pl.when(side > 0)(lambda: await_brick(jnp.maximum(side - 1, 0)))

        def put(at, inner):
            a, c = at // KB, lax.rem(at, KB)
            row, col = place(devices, order_ref, side, a, c)
            block = (aligned(row, FB), aligned(col, FB))
            piece = acc_ref[aligned(a, FB), aligned(c, FB)] * (64.0 / CELLS)
            seen = seen_ref[row * COLS + col]

            @pl.when(seen == 0)
            def _():
                sum_ref[block] = piece

            @pl.when(seen != 0)
            def _():
                sum_ref[block] += piece

            seen_ref[row * COLS + col] = 1
            pltpu.make_async_copy(sum_ref.at[block], ham_ref.at[block], ham_sems.at[side, a // 2]).start()
            return inner

        lax.fori_loop(0, count_ref[side] * KB, put, 0)
        return carry

    lax.fori_loop(0, 3, one_brick, 0)
    await_brick(2)


def f32(*shape):
    return jax.ShapeDtypeStruct(shape, jnp.float32)


def solution(mesh):
    devices = mesh.shape["dev"]

    def moved_by(value, steps):
        return lax.ppermute(value, "dev", [(i, (i + steps) % devices) for i in range(devices)])

    shared_scratch = [
        pltpu.SMEM((3 * KB,), jnp.int32),
        pltpu.SMEM((3,), jnp.int32),
        pltpu.VMEM((4, TILES * TILE, FB), jnp.float32),
        pltpu.VMEM((SIDE, WIDE), jnp.float32),
        pltpu.VMEM((SIDE, WIDE), jnp.float32),
        pltpu.VMEM((SIDE, WIDE), jnp.float32),
        pltpu.VMEM((CHUNK, WIDE), jnp.bfloat16),
        pltpu.VMEM((CHUNK, WIDE), jnp.bfloat16),
    ]

    def local(density_rows, center_x, center_y, center_z, exponent, brick_blocks):
        tables = [t.reshape(-1, FB) for t in (center_x, center_y, center_z, exponent)]
        bricks = brick_blocks.T
        to_left, kept, to_right, zeroed = pl.pallas_call(
            lambda *refs: density_kernel(devices, *refs),
            out_shape=[f32(1, CELLS + FB)] * 3 + [f32(BLK_DEV * FB, COLS * FB)],
            in_specs=[SMEM] + [HBM] * 5,
            out_specs=[VMEM] * 3 + [HBM],
            scratch_shapes=shared_scratch
            + [
                pltpu.VMEM((3, 2 * PAIR, WIDE), jnp.bfloat16),
                pltpu.VMEM((FB, COLS * FB), jnp.float32),
                pltpu.VMEM((3, 1, CELLS), jnp.float32),
                pltpu.SemaphoreType.DMA(()),
                pltpu.SemaphoreType.DMA((3, 2)),
                pltpu.SemaphoreType.DMA((BLK_DEV,)),
            ],
            compiler_params=pltpu.CompilerParams(vmem_limit_bytes=LIMIT),
        )(bricks, *tables, density_rows)
        from_right = moved_by(to_left, -1)
        from_left = moved_by(to_right, 1)
        density, head, tail = pl.pallas_call(
            add_kernel,
            out_shape=[f32(1, CELLS), f32(1, LAYER), f32(1, LAYER + FB)],
            in_specs=[VMEM] * 3,
            out_specs=[VMEM] * 3,
        )(kept, from_left, from_right)
        before = moved_by(tail, 2)
        left = moved_by(density, 1)
        right = moved_by(density, -1)
        after = moved_by(head, -2)
        charge = tail[:, LAYER:] + before[:, LAYER:]
        steps = 4
        while steps < devices:
            charge = charge + moved_by(charge, steps)
            steps *= 2
        return pl.pallas_call(
            lambda *refs: ham_kernel(devices, *refs),
            out_shape=[f32(1, CELLS), f32(BLK_DEV * FB, COLS * FB)],
            in_specs=[SMEM] + [HBM] * 4 + [VMEM] * 6 + [HBM],
            out_specs=[VMEM, HBM],
            scratch_shapes=shared_scratch
            + [
                pltpu.VMEM((3, 8, CELLS), jnp.float32),
                pltpu.VMEM((2 * PAIR, WIDE), jnp.float32),
                pltpu.VMEM((BLK_DEV * FB, COLS * FB), jnp.float32),
                pltpu.SMEM((BLK_DEV * COLS,), jnp.int32),
                pltpu.SemaphoreType.DMA(()),
                pltpu.SemaphoreType.DMA((3, 2)),
            ],
            input_output_aliases={11: 1},
            compiler_params=pltpu.CompilerParams(vmem_limit_bytes=LIMIT),
        )(bricks, *tables, left, density, right, before, after, charge, zeroed)

    return jax.shard_map(
        local,
        mesh=mesh,
        in_specs=(P("dev", None), P(), P(), P(), P(), P()),
        out_specs=(P("dev", None), P("dev", None)),
        check_vma=False,
    )
```

```python
import math

import jax
import jax.numpy as jnp
from jax import lax
from jax.experimental import pallas as pl
from jax.experimental.pallas import tpu as pltpu
from jax.sharding import PartitionSpec as P

FB = 128
KB = 8
BLK_DEV = 6
SIDE = 16
LAYER = SIDE * SIDE
CELLS = SIDE * LAYER
WIDE = KB * FB
CHUNK = 1024
SUB = 256
PAIR = 2 * FB
TILE = 8
TILES = 5
COLS = 5 * BLK_DEV

omega = 2.0 / 3.0
four_pi = 4.0 * math.pi
slater = (3.0 / math.pi) ** (1.0 / 3.0)

VMEM = pl.BlockSpec(memory_space=pltpu.VMEM)
SMEM = pl.BlockSpec(memory_space=pltpu.SMEM)
HBM = pl.BlockSpec(memory_space=pltpu.HBM)
LIMIT = 63 * 2**20


def aligned(index, unit):
    return pl.ds(pl.multiple_of(index * unit, unit), unit)


def wrap(value, count):
    return lax.rem(value + 2 * count, count)


def list_blocks(devices, bricks_ref, order_ref, count_ref):
    own = lax.axis_index("dev")
    for side in range(3):
        brick = wrap(own + side - 1, devices)
        ids = [bricks_ref[k, brick] for k in range(KB)]
        held = [(i // BLK_DEV == own).astype(jnp.int32) for i in ids]
        first, second = jnp.int32(0), sum(held)
        count_ref[side] = second
        for i, h in zip(ids, held):
            order_ref[side * KB + jnp.where(h == 1, first, second)] = i
            first, second = first + h, second + 1 - h


def place(devices, order_ref, side, a, c):
    own = lax.axis_index("dev")
    row_block, col_block = order_ref[side * KB + a], order_ref[side * KB + c]
    col = wrap(col_block // BLK_DEV - own + 2, devices) * BLK_DEV + lax.rem(col_block, BLK_DEV)
    return lax.rem(row_block, BLK_DEV), col


def first_tile(devices):
    own = lax.axis_index("dev")
    return wrap((own - 2) * BLK_DEV, devices * BLK_DEV) // TILE


def fetch_tables(devices, table_refs, tables_ref, sem):
    base = first_tile(devices)
    for t, table_ref in enumerate(table_refs):
        for k in range(TILES):
            tile = lax.rem(base + k, devices * BLK_DEV // TILE)
            pltpu.make_async_copy(
                table_ref.at[aligned(tile, TILE), :], tables_ref.at[t, pl.ds(k * TILE, TILE), :], sem
            ).start()


def factors(devices, side, order_ref, tables_ref, x_ref, y_ref, z_ref):
    own = lax.axis_index("dev")
    brick = wrap(own + side - 1, devices)
    base = first_tile(devices) * TILE
    points = (lax.broadcasted_iota(jnp.int32, (SIDE, FB), 0).astype(jnp.float32) + 0.5) / SIDE
    for k in range(KB):
        block = order_ref[side * KB + k]
        offset = (wrap(brick - block // BLK_DEV + 1, devices) - 1).astype(jnp.float32)
        row = pl.ds(wrap(block - base, devices * BLK_DEV), 1)
        decay = -tables_ref[3, row, :]
        lanes = pl.ds(k * FB, FB)
        along_x = (offset + points) - tables_ref[0, row, :]
        x_ref[:, lanes] = jnp.exp(decay * along_x * along_x)
        for t, out_ref in ((1, y_ref), (2, z_ref)):
            away = points - tables_ref[t, row, :] + 0.5
            away = away - jnp.floor(away) - 0.5
            out_ref[:, lanes] = jnp.exp(decay * away * away)


def orbital_chunk(part, step, x_ref, y_ref, z_ref, orb_ref):
    layers = CHUNK // LAYER
    for k in range(KB):
        lanes = slice(k * FB, (k + 1) * FB)
        x = x_ref[aligned(step, 8), lanes]
        y, z = y_ref[:, lanes], z_ref[:, lanes]
        for i in range(layers):
            xy = x[part * layers + i : part * layers + i + 1] * y
            for j in range(SIDE):
                at = (i * SIDE + j) * SIDE
                orb_ref[at : at + SIDE, lanes] = (xy[j : j + 1] * z).astype(jnp.bfloat16)


def density_of(
    devices, sides, bricks_ref, table_refs, rows_ref,
    order_ref, count_ref, tables_ref, x_ref, y_ref, z_ref, orb_a, orb_b, dens_ref, res_ref, table_sem, dens_sems,
):
    first, stride = sides
    fetch_tables(devices, table_refs, tables_ref, table_sem)
    list_blocks(devices, bricks_ref, order_ref, count_ref)
    slots = dens_ref.shape[0]

    def fetch_brick(slot, carry):
        side = first + stride * slot

        def fetch(at, inner):
            a, c = at // KB, lax.rem(at, KB)
            row, col = place(devices, order_ref, side, a, c)
            pltpu.make_async_copy(
                rows_ref.at[aligned(row, FB), aligned(col, FB)],
                dens_ref.at[slot, aligned(a, FB), aligned(c, FB)],
                dens_sems.at[slot, a // 2],
            ).start()
            return inner

        return lax.fori_loop(0, count_ref[side] * KB, fetch, carry)

    lax.fori_loop(0, slots, fetch_brick, 0)
    pltpu.make_async_copy(tables_ref, tables_ref, table_sem).wait()

    def one_brick(slot, carry):
        side = first + stride * slot
        factors(devices, side, order_ref, tables_ref, x_ref, y_ref, z_ref)

        def await_half(half, inner):
            pltpu.make_async_copy(
                rows_ref.at[pl.ds(0, PAIR), pl.ds(0, WIDE)],
                dens_ref.at[slot, aligned(half, PAIR), :],
                dens_sems.at[slot, half],
            ).wait()
            return inner

        lax.fori_loop(0, count_ref[side] // 2, await_half, 0)

        def steps(rows):
            def step(t, inner):
                for part, orb_ref in ((0, orb_a), (1, orb_b)):
                    orbital_chunk(part, t, x_ref, y_ref, z_ref, orb_ref)
                    for s in range(0, CHUNK, SUB):
                        applied = lax.dot_general(
                            orb_ref[s : s + SUB, :], dens_ref[slot, :rows, :], (((1,), (1,)), ((), ())),
                            preferred_element_type=jnp.float32,
                        )
                        product = applied * orb_ref[s : s + SUB, :rows].astype(jnp.float32)
                        total = product[:, :FB]
                        for k in range(FB, rows, FB):
                            total = total + product[:, k : k + FB]
                        at = pl.ds(pl.multiple_of(t * 2 * CHUNK + part * CHUNK + s, SUB), SUB)
                        res_ref[slot, :, at] = jnp.sum(total.T, axis=0, keepdims=True)
                return inner

            lax.fori_loop(0, CELLS // (2 * CHUNK), step, 0)

        pl.when(count_ref[side] == 2)(lambda: steps(PAIR))
        pl.when(count_ref[side] != 2)(lambda: steps(2 * PAIR))
        return carry

    lax.fori_loop(0, slots, one_brick, 0)


def folded(row):
    total = row[:, :FB]
    for k in range(1, CELLS // FB):
        total = total + row[:, k * FB : (k + 1) * FB]
    return total


def odd_device():
    return lax.rem(lax.axis_index("dev"), 2)


def beside_kernel(devices, bricks_ref, cx_ref, cy_ref, cz_ref, ex_ref, rows_ref, mate_ref, far_ref, charge_ref, *scratch):
    density_of(devices, (0, 2), bricks_ref, (cx_ref, cy_ref, cz_ref, ex_ref), rows_ref, *scratch)
    res_ref = scratch[9]
    odd = odd_device()
    mate_ref[...] = res_ref[1 - odd]
    far_ref[...] = res_ref[odd]
    charge_ref[...] = folded(res_ref[0] + res_ref[1])


def own_kernel(
    devices, bricks_ref, cx_ref, cy_ref, cz_ref, ex_ref, rows_ref, mate_ref, charge_ref,
    pack_ref, charges_ref, zero_out_ref, *scratch
):
    zero_ref, zero_sems = scratch[-2:]
    zero_ref[...] = jnp.zeros_like(zero_ref)
    zero_copies = [
        pltpu.make_async_copy(zero_ref, zero_out_ref.at[pl.ds(r * FB, FB), :], zero_sems.at[r]) for r in range(BLK_DEV)
    ]
    for copy in zero_copies:
        copy.start()
    density_of(devices, (1, 0), bricks_ref, (cx_ref, cy_ref, cz_ref, ex_ref), rows_ref, *scratch[:-2])
    res_ref = scratch[9]
    pack_ref[:, :CELLS] = mate_ref[...]
    pack_ref[:, CELLS:] = res_ref[0]
    charge = charge_ref[...] + folded(res_ref[0])
    charges_ref[...] = jnp.broadcast_to(charge[None], charges_ref.shape)
    for copy in zero_copies:
        copy.wait()


def add_kernel(pack_ref, mate_pack_ref, far_ref, mate_far_ref, own_ref, mate_ref):
    own = pack_ref[:, CELLS:] + mate_pack_ref[:, :CELLS] + far_ref[...]
    mate = pack_ref[:, :CELLS] + mate_pack_ref[:, CELLS:] + mate_far_ref[...]
    own_ref[:, :CELLS] = own
    own_ref[:, CELLS:] = jnp.where(odd_device() == 1, mate[:, CELLS - LAYER :], mate[:, :LAYER])
    mate_ref[...] = mate


def potential_of(density, before, after, average):
    lane = lax.broadcasted_iota(jnp.int32, density.shape, 1)
    along_z = lane & (SIDE - 1)
    along_y = (lane // SIDE) & (SIDE - 1)
    scale = omega * four_pi / 6.0
    source = density - average
    one = scale * source
    padded = jnp.concatenate([scale * (before - average), one, scale * (after - average)], axis=1)
    beside = padded[:, :CELLS] + padded[:, 2 * LAYER :]

    def moved(steps):
        return pltpu.roll(one, steps % CELLS, 1)

    beside += jnp.where(along_y > 0, moved(SIDE), moved(SIDE - LAYER))
    beside += jnp.where(along_y < SIDE - 1, moved(-SIDE), moved(LAYER - SIDE))
    beside += jnp.where(along_z > 0, moved(1), moved(1 - SIDE))
    beside += jnp.where(along_z < SIDE - 1, moved(-1), moved(SIDE - 1))
    two = one + omega * ((four_pi * source + beside) / 6.0 - one)
    root = jnp.exp(jnp.log(jnp.abs(density)) * (1.0 / 3.0))
    return two - slater * jnp.where(density < 0.0, -root, root)


def ham_kernel(
    devices, bricks_ref, cx_ref, cy_ref, cz_ref, ex_ref,
    own_ref, mate_ref, far_ref, mate_far_ref, charges_ref, zeroed_ref,
    pot_ref, ham_ref,
    order_ref, count_ref, tables_ref, x_ref, y_ref, z_ref, orb_a, orb_b, v_ref, acc_ref, sum_ref, seen_ref,
    table_sem, ham_sems,
):
    fetch_tables(devices, (cx_ref, cy_ref, cz_ref, ex_ref), tables_ref, table_sem)
    list_blocks(devices, bricks_ref, order_ref, count_ref)

    def clear(at, carry):
        seen_ref[at] = 0
        return carry

    lax.fori_loop(0, BLK_DEV * COLS, clear, 0)

    def wide(row):
        return jnp.broadcast_to(row, (8, row.shape[1]))

    odd = odd_device() == 1
    mate, far = mate_ref[...], far_ref[:, :CELLS]
    far_edge, mate_edge = far_ref[:, CELLS:], jnp.where(odd, mate_far_ref[:, CELLS - LAYER : CELLS], mate_far_ref[:, :LAYER])
    mid = wide(own_ref[:, :CELLS])
    left, right = wide(jnp.where(odd, mate, far)), wide(jnp.where(odd, far, mate))
    before, after = wide(jnp.where(odd, mate_edge, far_edge)), wide(jnp.where(odd, far_edge, mate_edge))
    average = jnp.sum(jnp.sum(charges_ref[...], axis=0)) / (devices * CELLS)
    v_ref[0] = potential_of(left, before, mid[:, :LAYER], average)
    own_potential = potential_of(mid, left[:, CELLS - LAYER :], right[:, :LAYER], average)
    v_ref[1] = own_potential
    v_ref[2] = potential_of(right, mid[:, CELLS - LAYER :], after, average)
    pot_ref[...] = own_potential[:1]
    pltpu.make_async_copy(tables_ref, tables_ref, table_sem).wait()

    def await_rows(side, rows_half):
        pltpu.make_async_copy(
            sum_ref.at[pl.ds(0, PAIR), pl.ds(0, WIDE)], ham_ref.at[pl.ds(0, PAIR), pl.ds(0, WIDE)],
            ham_sems.at[side, rows_half],
        ).wait()

    def await_brick(side):
        lax.fori_loop(0, count_ref[side] // 2, lambda half, inner: (await_rows(side, half), inner)[1], 0)

    def one_brick(side, carry):
        factors(devices, side, order_ref, tables_ref, x_ref, y_ref, z_ref)

        def steps(rows):
            def step(t, inner):
                for part, orb_ref in ((0, orb_a), (1, orb_b)):
                    orbital_chunk(part, t, x_ref, y_ref, z_ref, orb_ref)
                    at = pl.ds(pl.multiple_of(t * 2 * CHUNK + part * CHUNK, CHUNK), CHUNK)
                    v = v_ref[side, pl.ds(0, 1), at]
                    mine = orb_ref[:, :rows].T
                    weighted = (mine.astype(jnp.float32) * v).astype(jnp.bfloat16)
                    acc_ref[:rows, :] += jnp.dot(weighted, orb_ref[...], preferred_element_type=jnp.float32)
                return inner

            acc_ref[:rows, :] = jnp.zeros((rows, WIDE), jnp.float32)
            lax.fori_loop(0, CELLS // (2 * CHUNK), step, 0)

        pl.when(count_ref[side] == 2)(lambda: steps(PAIR))
        pl.when(count_ref[side] != 2)(lambda: steps(2 * PAIR))
        pl.when(side > 0)(lambda: await_brick(jnp.maximum(side - 1, 0)))

        def put(at, inner):
            a, c = at // KB, lax.rem(at, KB)
            row, col = place(devices, order_ref, side, a, c)
            block = (aligned(row, FB), aligned(col, FB))
            piece = acc_ref[aligned(a, FB), aligned(c, FB)] * (64.0 / CELLS)
            seen = seen_ref[row * COLS + col]

            @pl.when(seen == 0)
            def _():
                sum_ref[block] = piece

            @pl.when(seen != 0)
            def _():
                sum_ref[block] += piece

            seen_ref[row * COLS + col] = 1
            pltpu.make_async_copy(sum_ref.at[block], ham_ref.at[block], ham_sems.at[side, a // 2]).start()
            return inner

        lax.fori_loop(0, count_ref[side] * KB, put, 0)
        return carry

    lax.fori_loop(0, 3, one_brick, 0)
    await_brick(2)


def f32(*shape):
    return jax.ShapeDtypeStruct(shape, jnp.float32)


def solution(mesh):
    devices = mesh.shape["dev"]

    def with_mate(value):
        return lax.ppermute(value, "dev", [(i, i ^ 1) for i in range(devices)])

    def with_far(value):
        return lax.ppermute(value, "dev", [(i, (i + (i % 2) * 2 - 1) % devices) for i in range(devices)])

    shared_scratch = [
        pltpu.SMEM((3 * KB,), jnp.int32),
        pltpu.SMEM((3,), jnp.int32),
        pltpu.VMEM((4, TILES * TILE, FB), jnp.float32),
        pltpu.VMEM((SIDE, WIDE), jnp.float32),
        pltpu.VMEM((SIDE, WIDE), jnp.float32),
        pltpu.VMEM((SIDE, WIDE), jnp.float32),
        pltpu.VMEM((CHUNK, WIDE), jnp.bfloat16),
        pltpu.VMEM((CHUNK, WIDE), jnp.bfloat16),
    ]

    def local(density_rows, center_x, center_y, center_z, exponent, brick_blocks):
        tables = [t.reshape(-1, FB) for t in (center_x, center_y, center_z, exponent)]
        bricks = brick_blocks.T
        params = pltpu.CompilerParams(vmem_limit_bytes=LIMIT)

        def density_scratch(slots):
            return shared_scratch + [
                pltpu.VMEM((slots, 2 * PAIR, WIDE), jnp.bfloat16),
                pltpu.VMEM((slots, 1, CELLS), jnp.float32),
                pltpu.SemaphoreType.DMA(()),
                pltpu.SemaphoreType.DMA((slots, 2)),
            ]

        for_mate, for_far, charge = pl.pallas_call(
            lambda *refs: beside_kernel(devices, *refs),
            out_shape=[f32(1, CELLS), f32(1, CELLS), f32(1, FB)],
            in_specs=[SMEM] + [HBM] * 5,
            out_specs=[VMEM] * 3,
            scratch_shapes=density_scratch(2),
            compiler_params=params,
        )(bricks, *tables, density_rows)
        far_part = with_far(for_far)
        pack, charges, zeroed = pl.pallas_call(
            lambda *refs: own_kernel(devices, *refs),
            out_shape=[f32(1, 2 * CELLS), f32(devices, 1, FB), f32(BLK_DEV * FB, COLS * FB)],
            in_specs=[SMEM] + [HBM] * 5 + [VMEM] * 2,
            out_specs=[VMEM, VMEM, HBM],
            scratch_shapes=density_scratch(1)
            + [pltpu.VMEM((FB, COLS * FB), jnp.float32), pltpu.SemaphoreType.DMA((BLK_DEV,))],
            compiler_params=params,
            cost_estimate=pl.CostEstimate(flops=8 * 10**9, bytes_accessed=2 * 10**7, transcendentals=0),
        )(bricks, *tables, density_rows, for_mate, charge)
        charges = lax.all_to_all(charges, "dev", 0, 0, tiled=True)
        mate_pack = with_mate(pack)
        mate_far_part = with_mate(far_part)
        own, mate = pl.pallas_call(
            add_kernel,
            out_shape=[f32(1, CELLS + LAYER), f32(1, CELLS)],
            in_specs=[VMEM] * 4,
            out_specs=[VMEM] * 2,
        )(pack, mate_pack, far_part, mate_far_part)
        far = with_far(own)
        mate_far = with_mate(far)
        return pl.pallas_call(
            lambda *refs: ham_kernel(devices, *refs),
            out_shape=[f32(1, CELLS), f32(BLK_DEV * FB, COLS * FB)],
            in_specs=[SMEM] + [HBM] * 4 + [VMEM] * 5 + [HBM],
            out_specs=[VMEM, HBM],
            scratch_shapes=shared_scratch
            + [
                pltpu.VMEM((3, 8, CELLS), jnp.float32),
                pltpu.VMEM((2 * PAIR, WIDE), jnp.float32),
                pltpu.VMEM((BLK_DEV * FB, COLS * FB), jnp.float32),
                pltpu.SMEM((BLK_DEV * COLS,), jnp.int32),
                pltpu.SemaphoreType.DMA(()),
                pltpu.SemaphoreType.DMA((3, 2)),
            ],
            input_output_aliases={10: 1},
            compiler_params=params,
        )(bricks, *tables, own, mate, far, mate_far, charges, zeroed)

    return jax.shard_map(
        local,
        mesh=mesh,
        in_specs=(P("dev", None), P(), P(), P(), P(), P()),
        out_specs=(P("dev", None), P("dev", None)),
        check_vma=False,
    )
```

```python
import math

import jax
import jax.numpy as jnp
from jax import lax
from jax.experimental import pallas as pl
from jax.experimental.pallas import tpu as pltpu
from jax.sharding import PartitionSpec as P

FB = 128
KB = 8
BLK_DEV = 6
SIDE = 16
LAYER = SIDE * SIDE
CELLS = SIDE * LAYER
WIDE = KB * FB
CHUNK = 1024
SUB = 256
PAIR = 2 * FB
TILE = 8
TILES = 5
COLS = 5 * BLK_DEV

omega = 2.0 / 3.0
four_pi = 4.0 * math.pi
slater = (3.0 / math.pi) ** (1.0 / 3.0)

VMEM = pl.BlockSpec(memory_space=pltpu.VMEM)
SMEM = pl.BlockSpec(memory_space=pltpu.SMEM)
HBM = pl.BlockSpec(memory_space=pltpu.HBM)
LIMIT = 63 * 2**20


def aligned(index, unit):
    return pl.ds(pl.multiple_of(index * unit, unit), unit)


def wrap(value, count):
    return lax.rem(value + 2 * count, count)


def list_blocks(devices, sides, bricks_ref, lists_ref, count_ref):
    own = lax.axis_index("dev")
    for side in sides:
        brick = wrap(own + side - 1, devices)
        ids = [bricks_ref[k, brick] for k in range(KB)]
        owners = [i // BLK_DEV for i in ids]
        held = [(owner == own).astype(jnp.int32) for owner in owners]
        first, second = jnp.int32(0), sum(held)
        count_ref[side] = second
        for i, owner, h in zip(ids, owners, held):
            at = side * KB + jnp.where(h == 1, first, second)
            row = i - owner * BLK_DEV
            lists_ref[0, at] = i
            lists_ref[1, at] = row
            lists_ref[2, at] = wrap(owner - own + 2, devices) * BLK_DEV + row
            lists_ref[3, at] = owner
            first, second = first + h, second + 1 - h


def first_tile(devices):
    own = lax.axis_index("dev")
    return wrap((own - 2) * BLK_DEV, devices * BLK_DEV) // TILE


def fetch_tables(devices, table_refs, tables_ref, sem):
    base = first_tile(devices)
    for t, table_ref in enumerate(table_refs):
        for k in range(TILES):
            tile = lax.rem(base + k, devices * BLK_DEV // TILE)
            pltpu.make_async_copy(
                table_ref.at[aligned(tile, TILE), :], tables_ref.at[t, pl.ds(k * TILE, TILE), :], sem
            ).start()


def factors(devices, side, lists_ref, tables_ref, x_ref, y_ref, z_ref):
    own = lax.axis_index("dev")
    brick = wrap(own + side - 1, devices)
    base = first_tile(devices) * TILE
    points = (lax.broadcasted_iota(jnp.int32, (SIDE, FB), 0).astype(jnp.float32) + 0.5) / SIDE
    for k in range(KB):
        block, owner = lists_ref[0, side * KB + k], lists_ref[3, side * KB + k]
        offset = (wrap(brick - owner + 1, devices) - 1).astype(jnp.float32)
        row = pl.ds(wrap(block - base, devices * BLK_DEV), 1)
        decay = -tables_ref[3, row, :]
        lanes = pl.ds(k * FB, FB)
        along_x = (offset + points) - tables_ref[0, row, :]
        x_ref[:, lanes] = jnp.exp(decay * along_x * along_x)
        for t, out_ref in ((1, y_ref), (2, z_ref)):
            away = points - tables_ref[t, row, :] + 0.5
            away = away - jnp.floor(away) - 0.5
            out_ref[:, lanes] = jnp.exp(decay * away * away)


def orbital_chunk(part, step, x_ref, y_ref, z_ref, orb_ref):
    layers = CHUNK // LAYER
    for k in range(KB):
        lanes = slice(k * FB, (k + 1) * FB)
        x = x_ref[aligned(step, 8), lanes]
        y, z = y_ref[:, lanes], z_ref[:, lanes]
        for i in range(layers):
            xy = x[part * layers + i : part * layers + i + 1] * y
            for j in range(SIDE):
                at = (i * SIDE + j) * SIDE
                orb_ref[at : at + SIDE, lanes] = (xy[j : j + 1] * z).astype(jnp.bfloat16)


def density_of(
    devices, sides, bricks_ref, table_refs, rows_ref,
    lists_ref, count_ref, tables_ref, x_ref, y_ref, z_ref, orb_a, orb_b, dens_ref, res_ref, table_sem, dens_sems,
):
    first, stride = sides
    fetch_tables(devices, table_refs, tables_ref, table_sem)
    slots = dens_ref.shape[0]
    list_blocks(devices, [first + stride * slot for slot in range(slots)], bricks_ref, lists_ref, count_ref)

    def fetch_brick(slot, carry):
        side = first + stride * slot

        def fetch(half, inner):
            for a in range(2):
                row = lists_ref[1, side * KB + half * 2 + a]
                for c in range(KB):
                    pltpu.make_async_copy(
                        rows_ref.at[aligned(row, FB), aligned(lists_ref[2, side * KB + c], FB)],
                        dens_ref.at[slot, aligned(half * 2 + a, FB), pl.ds(c * FB, FB)],
                        dens_sems.at[slot, half],
                    ).start()
            return inner

        return lax.fori_loop(0, count_ref[side] // 2, fetch, carry)

    lax.fori_loop(0, slots, fetch_brick, 0)
    pltpu.make_async_copy(tables_ref, tables_ref, table_sem).wait()

    def one_brick(slot, carry):
        side = first + stride * slot
        factors(devices, side, lists_ref, tables_ref, x_ref, y_ref, z_ref)

        def await_half(half, inner):
            pltpu.make_async_copy(
                rows_ref.at[pl.ds(0, PAIR), pl.ds(0, WIDE)],
                dens_ref.at[slot, aligned(half, PAIR), :],
                dens_sems.at[slot, half],
            ).wait()
            return inner

        lax.fori_loop(0, count_ref[side] // 2, await_half, 0)

        def steps(rows):
            def step(t, inner):
                for part, orb_ref in ((0, orb_a), (1, orb_b)):
                    orbital_chunk(part, t, x_ref, y_ref, z_ref, orb_ref)
                    for s in range(0, CHUNK, SUB):
                        applied = lax.dot_general(
                            orb_ref[s : s + SUB, :], dens_ref[slot, :rows, :], (((1,), (1,)), ((), ())),
                            preferred_element_type=jnp.float32,
                        )
                        product = applied * orb_ref[s : s + SUB, :rows].astype(jnp.float32)
                        total = product[:, :FB]
                        for k in range(FB, rows, FB):
                            total = total + product[:, k : k + FB]
                        at = pl.ds(pl.multiple_of(t * 2 * CHUNK + part * CHUNK + s, SUB), SUB)
                        res_ref[slot, :, at] = jnp.sum(total.T, axis=0, keepdims=True)
                return inner

            lax.fori_loop(0, CELLS // (2 * CHUNK), step, 0)

        pl.when(count_ref[side] == 2)(lambda: steps(PAIR))
        pl.when(count_ref[side] != 2)(lambda: steps(2 * PAIR))
        return carry

    lax.fori_loop(0, slots, one_brick, 0)


def folded(row):
    total = row[:, :FB]
    for k in range(1, CELLS // FB):
        total = total + row[:, k * FB : (k + 1) * FB]
    return total


def odd_device():
    return lax.rem(lax.axis_index("dev"), 2)


def beside_kernel(devices, bricks_ref, cx_ref, cy_ref, cz_ref, ex_ref, rows_ref, mate_ref, far_ref, charge_ref, *scratch):
    density_of(devices, (0, 2), bricks_ref, (cx_ref, cy_ref, cz_ref, ex_ref), rows_ref, *scratch)
    res_ref = scratch[9]
    odd = odd_device()
    mate_ref[...] = res_ref[1 - odd]
    far_ref[...] = res_ref[odd]
    charge_ref[...] = folded(res_ref[0] + res_ref[1])


def own_kernel(
    devices, bricks_ref, cx_ref, cy_ref, cz_ref, ex_ref, rows_ref, mate_ref, charge_ref,
    pack_ref, total_ref, zero_out_ref, *scratch
):
    zero_ref, zero_sems = scratch[-2:]
    zero_ref[...] = jnp.zeros_like(zero_ref)
    zero_copies = [
        pltpu.make_async_copy(zero_ref, zero_out_ref.at[pl.ds(r * FB, FB), :], zero_sems.at[r]) for r in range(BLK_DEV)
    ]
    for copy in zero_copies:
        copy.start()
    density_of(devices, (1, 0), bricks_ref, (cx_ref, cy_ref, cz_ref, ex_ref), rows_ref, *scratch[:-2])
    res_ref = scratch[9]
    pack_ref[:, :CELLS] = mate_ref[...]
    pack_ref[:, CELLS:] = res_ref[0]
    total_ref[...] = charge_ref[...] + folded(res_ref[0])
    for copy in zero_copies:
        copy.wait()


def add_kernel(pack_ref, mate_pack_ref, far_ref, mate_far_ref, total_ref, own_ref, mate_ref, charges_ref):
    own = pack_ref[:, CELLS:] + mate_pack_ref[:, :CELLS] + far_ref[...]
    mate = pack_ref[:, :CELLS] + mate_pack_ref[:, CELLS:] + mate_far_ref[...]
    own_ref[:, :CELLS] = own
    own_ref[:, CELLS:] = jnp.where(odd_device() == 1, mate[:, CELLS - LAYER :], mate[:, :LAYER])
    mate_ref[...] = mate
    charges_ref[...] = jnp.broadcast_to(total_ref[...][None], charges_ref.shape)


def potential_of(density, before, after, average):
    lane = lax.broadcasted_iota(jnp.int32, density.shape, 1)
    along_z = lane & (SIDE - 1)
    along_y = (lane // SIDE) & (SIDE - 1)
    scale = omega * four_pi / 6.0
    source = density - average
    one = scale * source
    padded = jnp.concatenate([scale * (before - average), one, scale * (after - average)], axis=1)
    beside = padded[:, :CELLS] + padded[:, 2 * LAYER :]

    def moved(steps):
        return pltpu.roll(one, steps % CELLS, 1)

    beside += jnp.where(along_y > 0, moved(SIDE), moved(SIDE - LAYER))
    beside += jnp.where(along_y < SIDE - 1, moved(-SIDE), moved(LAYER - SIDE))
    beside += jnp.where(along_z > 0, moved(1), moved(1 - SIDE))
    beside += jnp.where(along_z < SIDE - 1, moved(-1), moved(SIDE - 1))
    two = one + omega * ((four_pi * source + beside) / 6.0 - one)
    root = jnp.exp(jnp.log(jnp.abs(density)) * (1.0 / 3.0))
    return two - slater * jnp.where(density < 0.0, -root, root)


def ham_kernel(
    devices, bricks_ref, cx_ref, cy_ref, cz_ref, ex_ref,
    own_ref, mate_ref, far_ref, mate_far_ref, charges_ref, zeroed_ref,
    pot_ref, ham_ref,
    lists_ref, count_ref, tables_ref, x_ref, y_ref, z_ref, orb_a, orb_b, v_ref, acc_ref, sum_ref,
    table_sem, ham_sems, clear_sem,
):
    fetch_tables(devices, (cx_ref, cy_ref, cz_ref, ex_ref), tables_ref, table_sem)
    clearing = pltpu.make_async_copy(ham_ref, sum_ref, clear_sem)
    clearing.start()
    list_blocks(devices, range(3), bricks_ref, lists_ref, count_ref)

    def wide(row):
        return jnp.broadcast_to(row, (8, row.shape[1]))

    odd = odd_device() == 1
    mate, far = mate_ref[...], far_ref[:, :CELLS]
    far_edge, mate_edge = far_ref[:, CELLS:], jnp.where(odd, mate_far_ref[:, CELLS - LAYER : CELLS], mate_far_ref[:, :LAYER])
    mid = wide(own_ref[:, :CELLS])
    left, right = wide(jnp.where(odd, mate, far)), wide(jnp.where(odd, far, mate))
    before, after = wide(jnp.where(odd, mate_edge, far_edge)), wide(jnp.where(odd, far_edge, mate_edge))
    average = jnp.sum(jnp.sum(charges_ref[...], axis=0)) / (devices * CELLS)
    scale = 64.0 / CELLS
    v_ref[0] = scale * potential_of(left, before, mid[:, :LAYER], average)
    own_potential = potential_of(mid, left[:, CELLS - LAYER :], right[:, :LAYER], average)
    v_ref[1] = scale * own_potential
    v_ref[2] = scale * potential_of(right, mid[:, CELLS - LAYER :], after, average)
    pot_ref[...] = own_potential[:1]
    pltpu.make_async_copy(tables_ref, tables_ref, table_sem).wait()

    def await_rows(side, rows_half):
        pltpu.make_async_copy(
            sum_ref.at[pl.ds(0, PAIR), pl.ds(0, WIDE)], ham_ref.at[pl.ds(0, PAIR), pl.ds(0, WIDE)],
            ham_sems.at[side, rows_half],
        ).wait()

    def await_brick(side):
        lax.fori_loop(0, count_ref[side] // 2, lambda half, inner: (await_rows(side, half), inner)[1], 0)

    def one_brick(side, carry):
        factors(devices, side, lists_ref, tables_ref, x_ref, y_ref, z_ref)

        def steps(rows):
            def step(t, inner):
                for part, orb_ref in ((0, orb_a), (1, orb_b)):
                    orbital_chunk(part, t, x_ref, y_ref, z_ref, orb_ref)
                    at = pl.ds(pl.multiple_of(t * 2 * CHUNK + part * CHUNK, CHUNK), CHUNK)
                    v = v_ref[side, pl.ds(0, 1), at]
                    mine = orb_ref[:, :rows].T
                    weighted = (mine.astype(jnp.float32) * v).astype(jnp.bfloat16)
                    acc_ref[:rows, :] += jnp.dot(weighted, orb_ref[...], preferred_element_type=jnp.float32)
                return inner

            acc_ref[:rows, :] = jnp.zeros((rows, WIDE), jnp.float32)
            lax.fori_loop(0, CELLS // (2 * CHUNK), step, 0)
            pl.when(side == 0)(clearing.wait)
            pl.when(side > 0)(lambda: await_brick(jnp.maximum(side - 1, 0)))
            for a in range(rows // FB):
                row = lists_ref[1, side * KB + a]
                for c in range(KB):
                    block = (aligned(row, FB), aligned(lists_ref[2, side * KB + c], FB))
                    sum_ref[block] += acc_ref[a * FB : (a + 1) * FB, c * FB : (c + 1) * FB]
                    pltpu.make_async_copy(sum_ref.at[block], ham_ref.at[block], ham_sems.at[side, a // 2]).start()

        pl.when(count_ref[side] == 2)(lambda: steps(PAIR))
        pl.when(count_ref[side] != 2)(lambda: steps(2 * PAIR))
        return carry

    lax.fori_loop(0, 3, one_brick, 0)
    await_brick(2)


def f32(*shape):
    return jax.ShapeDtypeStruct(shape, jnp.float32)


def solution(mesh):
    devices = mesh.shape["dev"]

    def with_mate(value):
        return lax.ppermute(value, "dev", [(i, i ^ 1) for i in range(devices)])

    def with_far(value):
        return lax.ppermute(value, "dev", [(i, (i + (i % 2) * 2 - 1) % devices) for i in range(devices)])

    shared_scratch = [
        pltpu.SMEM((4, 3 * KB), jnp.int32),
        pltpu.SMEM((3,), jnp.int32),
        pltpu.VMEM((4, TILES * TILE, FB), jnp.float32),
        pltpu.VMEM((SIDE, WIDE), jnp.float32),
        pltpu.VMEM((SIDE, WIDE), jnp.float32),
        pltpu.VMEM((SIDE, WIDE), jnp.float32),
        pltpu.VMEM((CHUNK, WIDE), jnp.bfloat16),
        pltpu.VMEM((CHUNK, WIDE), jnp.bfloat16),
    ]

    def local(density_rows, center_x, center_y, center_z, exponent, brick_blocks):
        tables = [t.reshape(-1, FB) for t in (center_x, center_y, center_z, exponent)]
        bricks = brick_blocks.T
        params = pltpu.CompilerParams(vmem_limit_bytes=LIMIT)

        def density_scratch(slots):
            return shared_scratch + [
                pltpu.VMEM((slots, 2 * PAIR, WIDE), jnp.bfloat16),
                pltpu.VMEM((slots, 1, CELLS), jnp.float32),
                pltpu.SemaphoreType.DMA(()),
                pltpu.SemaphoreType.DMA((slots, 2)),
            ]

        for_mate, for_far, charge = pl.pallas_call(
            lambda *refs: beside_kernel(devices, *refs),
            out_shape=[f32(1, CELLS), f32(1, CELLS), f32(1, FB)],
            in_specs=[SMEM] + [HBM] * 5,
            out_specs=[VMEM] * 3,
            scratch_shapes=density_scratch(2),
            compiler_params=params,
        )(bricks, *tables, density_rows)
        far_part = with_far(for_far)
        pack, total, zeroed = pl.pallas_call(
            lambda *refs: own_kernel(devices, *refs),
            out_shape=[f32(1, 2 * CELLS), f32(1, FB), f32(BLK_DEV * FB, COLS * FB)],
            in_specs=[SMEM] + [HBM] * 5 + [VMEM] * 2,
            out_specs=[VMEM, VMEM, HBM],
            scratch_shapes=density_scratch(1)
            + [pltpu.VMEM((FB, COLS * FB), jnp.float32), pltpu.SemaphoreType.DMA((BLK_DEV,))],
            compiler_params=params,
            cost_estimate=pl.CostEstimate(flops=8 * 10**9, bytes_accessed=2 * 10**7, transcendentals=0),
        )(bricks, *tables, density_rows, for_mate, charge)
        mate_pack = with_mate(pack)
        mate_far_part = with_mate(far_part)
        own, mate, charges = pl.pallas_call(
            add_kernel,
            out_shape=[f32(1, CELLS + LAYER), f32(1, CELLS), f32(devices, 1, FB)],
            in_specs=[VMEM] * 5,
            out_specs=[VMEM] * 3,
            compiler_params=pltpu.CompilerParams(vmem_limit_bytes=8 * 2**20),
        )(pack, mate_pack, far_part, mate_far_part, total)
        far = with_far(own)
        charges = lax.all_to_all(charges, "dev", 0, 0, tiled=True)
        mate_far = with_mate(far)
        return pl.pallas_call(
            lambda *refs: ham_kernel(devices, *refs),
            out_shape=[f32(1, CELLS), f32(BLK_DEV * FB, COLS * FB)],
            in_specs=[SMEM] + [HBM] * 4 + [VMEM] * 5 + [HBM],
            out_specs=[VMEM, HBM],
            scratch_shapes=shared_scratch
            + [
                pltpu.VMEM((3, 8, CELLS), jnp.float32),
                pltpu.VMEM((2 * PAIR, WIDE), jnp.float32),
                pltpu.VMEM((BLK_DEV * FB, COLS * FB), jnp.float32),
                pltpu.SemaphoreType.DMA(()),
                pltpu.SemaphoreType.DMA((3, 2)),
                pltpu.SemaphoreType.DMA(()),
            ],
            input_output_aliases={10: 1},
            compiler_params=params,
        )(bricks, *tables, own, mate, far, mate_far, charges, zeroed)

    return jax.shard_map(
        local,
        mesh=mesh,
        in_specs=(P("dev", None), P(), P(), P(), P(), P()),
        out_specs=(P("dev", None), P("dev", None)),
        check_vma=False,
    )
```

```python
import math

import jax
import jax.numpy as jnp
from jax import lax
from jax.experimental import pallas as pl
from jax.experimental.pallas import tpu as pltpu
from jax.sharding import PartitionSpec as P

FB = 128
KB = 8
BLK_DEV = 6
SIDE = 16
LAYER = SIDE * SIDE
CELLS = SIDE * LAYER
WIDE = KB * FB
CHUNK = 1024
SUB = 256
PAIR = 2 * FB
TILE = 8
TILES = 5
COLS = 5 * BLK_DEV

omega = 2.0 / 3.0
four_pi = 4.0 * math.pi
slater = (3.0 / math.pi) ** (1.0 / 3.0)

VMEM = pl.BlockSpec(memory_space=pltpu.VMEM)
SMEM = pl.BlockSpec(memory_space=pltpu.SMEM)
HBM = pl.BlockSpec(memory_space=pltpu.HBM)
LIMIT = 536 * 2**20 // 10


def aligned(index, unit):
    return pl.ds(pl.multiple_of(index * unit, unit), unit)


def wrap(value, count):
    return lax.rem(value + 2 * count, count)


def list_blocks(devices, sides, bricks_ref, lists_ref, count_ref):
    own = lax.axis_index("dev")
    for side in sides:
        brick = wrap(own + side - 1, devices)
        ids = [bricks_ref[k, brick] for k in range(KB)]
        owners = [i // BLK_DEV for i in ids]
        held = [(owner == own).astype(jnp.int32) for owner in owners]
        first, second = jnp.int32(0), sum(held)
        count_ref[side] = second
        for i, owner, h in zip(ids, owners, held):
            at = side * KB + jnp.where(h == 1, first, second)
            row = i - owner * BLK_DEV
            lists_ref[0, at] = i
            lists_ref[1, at] = row
            lists_ref[2, at] = wrap(owner - own + 2, devices) * BLK_DEV + row
            lists_ref[3, at] = owner
            first, second = first + h, second + 1 - h


def first_tile(devices):
    own = lax.axis_index("dev")
    return wrap((own - 2) * BLK_DEV, devices * BLK_DEV) // TILE


def fetch_tables(devices, table_refs, tables_ref, sem):
    base = first_tile(devices)
    for t, table_ref in enumerate(table_refs):
        for k in range(TILES):
            tile = lax.rem(base + k, devices * BLK_DEV // TILE)
            pltpu.make_async_copy(
                table_ref.at[aligned(tile, TILE), :], tables_ref.at[t, pl.ds(k * TILE, TILE), :], sem
            ).start()


def factors(devices, side, lists_ref, tables_ref, x_ref, y_ref, z_ref):
    own = lax.axis_index("dev")
    brick = wrap(own + side - 1, devices)
    base = first_tile(devices) * TILE
    points = (lax.broadcasted_iota(jnp.int32, (SIDE, FB), 0).astype(jnp.float32) + 0.5) / SIDE
    for k in range(KB):
        block, owner = lists_ref[0, side * KB + k], lists_ref[3, side * KB + k]
        offset = (wrap(brick - owner + 1, devices) - 1).astype(jnp.float32)
        row = pl.ds(wrap(block - base, devices * BLK_DEV), 1)
        decay = -tables_ref[3, row, :]
        lanes = pl.ds(k * FB, FB)
        along_x = (offset + points) - tables_ref[0, row, :]
        x_ref[:, lanes] = jnp.exp(decay * along_x * along_x)
        for t, out_ref in ((1, y_ref), (2, z_ref)):
            away = points - tables_ref[t, row, :] + 0.5
            away = away - jnp.floor(away) - 0.5
            out_ref[:, lanes] = jnp.exp(decay * away * away)


def orbital_chunk(part, step, x_ref, y_ref, z_ref, orb_ref):
    layers = CHUNK // LAYER
    for k in range(KB):
        lanes = slice(k * FB, (k + 1) * FB)
        x = x_ref[aligned(step, 8), lanes]
        y, z = y_ref[:, lanes], z_ref[:, lanes]
        for i in range(layers):
            xy = x[part * layers + i : part * layers + i + 1] * y
            for j in range(SIDE):
                at = (i * SIDE + j) * SIDE
                orb_ref[at : at + SIDE, lanes] = (xy[j : j + 1] * z).astype(jnp.bfloat16)


def density_of(
    devices, sides, bricks_ref, table_refs, rows_ref,
    lists_ref, count_ref, tables_ref, x_ref, y_ref, z_ref, orb_a, orb_b, dens_ref, res_ref, table_sem, dens_sems,
):
    first, stride = sides
    fetch_tables(devices, table_refs, tables_ref, table_sem)
    slots = dens_ref.shape[0]
    list_blocks(devices, [first + stride * slot for slot in range(slots)], bricks_ref, lists_ref, count_ref)

    def fetch_brick(slot, carry):
        side = first + stride * slot

        def fetch(half, inner):
            for a in range(2):
                row = lists_ref[1, side * KB + half * 2 + a]
                for c in range(KB):
                    pltpu.make_async_copy(
                        rows_ref.at[aligned(row, FB), aligned(lists_ref[2, side * KB + c], FB)],
                        dens_ref.at[slot, aligned(half * 2 + a, FB), pl.ds(c * FB, FB)],
                        dens_sems.at[slot, half],
                    ).start()
            return inner

        return lax.fori_loop(0, count_ref[side] // 2, fetch, carry)

    lax.fori_loop(0, slots, fetch_brick, 0)
    pltpu.make_async_copy(tables_ref, tables_ref, table_sem).wait()

    def one_brick(slot, carry):
        side = first + stride * slot
        factors(devices, side, lists_ref, tables_ref, x_ref, y_ref, z_ref)

        def await_half(half, inner):
            pltpu.make_async_copy(
                rows_ref.at[pl.ds(0, PAIR), pl.ds(0, WIDE)],
                dens_ref.at[slot, aligned(half, PAIR), :],
                dens_sems.at[slot, half],
            ).wait()
            return inner

        lax.fori_loop(0, count_ref[side] // 2, await_half, 0)

        def steps(rows):
            def step(t, inner):
                for part, orb_ref in ((0, orb_a), (1, orb_b)):
                    orbital_chunk(part, t, x_ref, y_ref, z_ref, orb_ref)
                    for s in range(0, CHUNK, SUB):
                        applied = lax.dot_general(
                            orb_ref[s : s + SUB, :], dens_ref[slot, :rows, :], (((1,), (1,)), ((), ())),
                            preferred_element_type=jnp.float32,
                        )
                        product = applied * orb_ref[s : s + SUB, :rows].astype(jnp.float32)
                        total = product[:, :FB]
                        for k in range(FB, rows, FB):
                            total = total + product[:, k : k + FB]
                        at = pl.ds(pl.multiple_of(t * 2 * CHUNK + part * CHUNK + s, SUB), SUB)
                        res_ref[slot, :, at] = jnp.sum(total.T, axis=0, keepdims=True)
                return inner

            lax.fori_loop(0, CELLS // (2 * CHUNK), step, 0)

        pl.when(count_ref[side] == 2)(lambda: steps(PAIR))
        pl.when(count_ref[side] != 2)(lambda: steps(2 * PAIR))
        return carry

    lax.fori_loop(0, slots, one_brick, 0)


def folded(row):
    total = row[:, :FB]
    for k in range(1, CELLS // FB):
        total = total + row[:, k * FB : (k + 1) * FB]
    return total


def odd_device():
    return lax.rem(lax.axis_index("dev"), 2)


def beside_kernel(devices, bricks_ref, cx_ref, cy_ref, cz_ref, ex_ref, rows_ref, mate_ref, far_ref, charge_ref, *scratch):
    density_of(devices, (0, 2), bricks_ref, (cx_ref, cy_ref, cz_ref, ex_ref), rows_ref, *scratch)
    res_ref = scratch[9]
    odd = odd_device()
    mate_ref[...] = res_ref[1 - odd]
    far_ref[...] = res_ref[odd]
    charge_ref[...] = folded(res_ref[0] + res_ref[1])


def own_kernel(
    devices, bricks_ref, cx_ref, cy_ref, cz_ref, ex_ref, rows_ref, mate_ref, charge_ref,
    pack_ref, total_ref, zero_out_ref, *scratch
):
    zero_ref, zero_sems = scratch[-2:]
    zero_ref[...] = jnp.zeros_like(zero_ref)
    zero_copies = [
        pltpu.make_async_copy(zero_ref, zero_out_ref.at[pl.ds(r * FB, FB), :], zero_sems.at[r]) for r in range(BLK_DEV)
    ]
    for copy in zero_copies:
        copy.start()
    density_of(devices, (1, 0), bricks_ref, (cx_ref, cy_ref, cz_ref, ex_ref), rows_ref, *scratch[:-2])
    res_ref = scratch[9]
    pack_ref[:, :CELLS] = mate_ref[...]
    pack_ref[:, CELLS:] = res_ref[0]
    total_ref[...] = charge_ref[...] + folded(res_ref[0])
    for copy in zero_copies:
        copy.wait()


def add_kernel(pack_ref, mate_pack_ref, far_ref, mate_far_ref, total_ref, own_ref, mate_ref, charges_ref):
    own = pack_ref[:, CELLS:] + mate_pack_ref[:, :CELLS] + far_ref[...]
    mate = pack_ref[:, :CELLS] + mate_pack_ref[:, CELLS:] + mate_far_ref[...]
    own_ref[:, :CELLS] = own
    own_ref[:, CELLS:] = jnp.where(odd_device() == 1, mate[:, CELLS - LAYER :], mate[:, :LAYER])
    mate_ref[...] = mate
    charges_ref[...] = jnp.broadcast_to(total_ref[...][None], charges_ref.shape)


def potential_of(density, before, after, average):
    lane = lax.broadcasted_iota(jnp.int32, density.shape, 1)
    along_z = lane & (SIDE - 1)
    along_y = (lane // SIDE) & (SIDE - 1)
    scale = omega * four_pi / 6.0
    source = density - average
    one = scale * source
    padded = jnp.concatenate([scale * (before - average), one, scale * (after - average)], axis=1)
    beside = padded[:, :CELLS] + padded[:, 2 * LAYER :]

    def moved(steps):
        return pltpu.roll(one, steps % CELLS, 1)

    beside += jnp.where(along_y > 0, moved(SIDE), moved(SIDE - LAYER))
    beside += jnp.where(along_y < SIDE - 1, moved(-SIDE), moved(LAYER - SIDE))
    beside += jnp.where(along_z > 0, moved(1), moved(1 - SIDE))
    beside += jnp.where(along_z < SIDE - 1, moved(-1), moved(SIDE - 1))
    two = one + omega * ((four_pi * source + beside) / 6.0 - one)
    root = jnp.exp(jnp.log(jnp.abs(density)) * (1.0 / 3.0))
    return two - slater * jnp.where(density < 0.0, -root, root)


def ham_kernel(
    devices, bricks_ref, cx_ref, cy_ref, cz_ref, ex_ref,
    own_ref, mate_ref, far_ref, mate_far_ref, charges_ref, zeroed_ref,
    pot_ref, ham_ref,
    lists_ref, count_ref, tables_ref, x_ref, y_ref, z_ref, orb_a, orb_b, v_ref, acc_ref, sum_ref,
    table_sem, ham_sems, clear_sem,
):
    fetch_tables(devices, (cx_ref, cy_ref, cz_ref, ex_ref), tables_ref, table_sem)
    clearing = pltpu.make_async_copy(ham_ref, sum_ref, clear_sem)
    clearing.start()
    list_blocks(devices, range(3), bricks_ref, lists_ref, count_ref)

    def wide(row):
        return jnp.broadcast_to(row, (8, row.shape[1]))

    odd = odd_device() == 1
    mate, far = mate_ref[...], far_ref[:, :CELLS]
    far_edge, mate_edge = far_ref[:, CELLS:], jnp.where(odd, mate_far_ref[:, CELLS - LAYER : CELLS], mate_far_ref[:, :LAYER])
    mid = wide(own_ref[:, :CELLS])
    left, right = wide(jnp.where(odd, mate, far)), wide(jnp.where(odd, far, mate))
    before, after = wide(jnp.where(odd, mate_edge, far_edge)), wide(jnp.where(odd, far_edge, mate_edge))
    average = jnp.sum(jnp.sum(charges_ref[...], axis=0)) / (devices * CELLS)
    scale = 64.0 / CELLS
    v_ref[0] = scale * potential_of(left, before, mid[:, :LAYER], average)
    own_potential = potential_of(mid, left[:, CELLS - LAYER :], right[:, :LAYER], average)
    v_ref[1] = scale * own_potential
    v_ref[2] = scale * potential_of(right, mid[:, CELLS - LAYER :], after, average)
    pot_ref[...] = own_potential[:1]
    pltpu.make_async_copy(tables_ref, tables_ref, table_sem).wait()

    def await_rows(side, rows_half):
        pltpu.make_async_copy(
            sum_ref.at[pl.ds(0, PAIR), pl.ds(0, WIDE)], ham_ref.at[pl.ds(0, PAIR), pl.ds(0, WIDE)],
            ham_sems.at[side, rows_half],
        ).wait()

    def await_brick(side):
        lax.fori_loop(0, count_ref[side] // 2, lambda half, inner: (await_rows(side, half), inner)[1], 0)

    def one_brick(side, carry):
        factors(devices, side, lists_ref, tables_ref, x_ref, y_ref, z_ref)

        def steps(rows):
            def step(t, inner):
                for part, orb_ref in ((0, orb_a), (1, orb_b)):
                    orbital_chunk(part, t, x_ref, y_ref, z_ref, orb_ref)
                    at = pl.ds(pl.multiple_of(t * 2 * CHUNK + part * CHUNK, CHUNK), CHUNK)
                    v = v_ref[side, pl.ds(0, 1), at]
                    mine = orb_ref[:, :rows].T
                    weighted = (mine.astype(jnp.float32) * v).astype(jnp.bfloat16)
                    for r in range(0, rows, PAIR):
                        acc_ref[r : r + PAIR, r:] += jnp.dot(
                            weighted[r : r + PAIR], orb_ref[:, r:], preferred_element_type=jnp.float32
                        )
                return inner

            acc_ref[:rows, :] = jnp.zeros((rows, WIDE), jnp.float32)
            lax.fori_loop(0, CELLS // (2 * CHUNK), step, 0)
            if rows > PAIR:
                acc_ref[PAIR:rows, :PAIR] = acc_ref[:PAIR, PAIR:rows].T
            pl.when(side == 0)(clearing.wait)
            pl.when(side > 0)(lambda: await_brick(jnp.maximum(side - 1, 0)))
            for a in range(rows // FB):
                row = lists_ref[1, side * KB + a]
                for c in range(KB):
                    block = (aligned(row, FB), aligned(lists_ref[2, side * KB + c], FB))
                    sum_ref[block] += acc_ref[a * FB : (a + 1) * FB, c * FB : (c + 1) * FB]
                    pltpu.make_async_copy(sum_ref.at[block], ham_ref.at[block], ham_sems.at[side, a // 2]).start()

        pl.when(count_ref[side] == 2)(lambda: steps(PAIR))
        pl.when(count_ref[side] != 2)(lambda: steps(2 * PAIR))
        return carry

    lax.fori_loop(0, 3, one_brick, 0)
    await_brick(2)


def f32(*shape):
    return jax.ShapeDtypeStruct(shape, jnp.float32)


def solution(mesh):
    devices = mesh.shape["dev"]

    def with_mate(value):
        return lax.ppermute(value, "dev", [(i, i ^ 1) for i in range(devices)])

    def with_far(value):
        return lax.ppermute(value, "dev", [(i, (i + (i % 2) * 2 - 1) % devices) for i in range(devices)])

    shared_scratch = [
        pltpu.SMEM((4, 3 * KB), jnp.int32),
        pltpu.SMEM((3,), jnp.int32),
        pltpu.VMEM((4, TILES * TILE, FB), jnp.float32),
        pltpu.VMEM((SIDE, WIDE), jnp.float32),
        pltpu.VMEM((SIDE, WIDE), jnp.float32),
        pltpu.VMEM((SIDE, WIDE), jnp.float32),
        pltpu.VMEM((CHUNK, WIDE), jnp.bfloat16),
        pltpu.VMEM((CHUNK, WIDE), jnp.bfloat16),
    ]

    def local(density_rows, center_x, center_y, center_z, exponent, brick_blocks):
        tables = [t.reshape(-1, FB) for t in (center_x, center_y, center_z, exponent)]
        bricks = brick_blocks.T
        params = pltpu.CompilerParams(vmem_limit_bytes=LIMIT)

        def density_scratch(slots):
            return shared_scratch + [
                pltpu.VMEM((slots, 2 * PAIR, WIDE), jnp.bfloat16),
                pltpu.VMEM((slots, 1, CELLS), jnp.float32),
                pltpu.SemaphoreType.DMA(()),
                pltpu.SemaphoreType.DMA((slots, 2)),
            ]

        for_mate, for_far, charge = pl.pallas_call(
            lambda *refs: beside_kernel(devices, *refs),
            out_shape=[f32(1, CELLS), f32(1, CELLS), f32(1, FB)],
            in_specs=[SMEM] + [HBM] * 5,
            out_specs=[VMEM] * 3,
            scratch_shapes=density_scratch(2),
            compiler_params=params,
        )(bricks, *tables, density_rows)
        far_part = with_far(for_far)
        pack, total, zeroed = pl.pallas_call(
            lambda *refs: own_kernel(devices, *refs),
            out_shape=[f32(1, 2 * CELLS), f32(1, FB), f32(BLK_DEV * FB, COLS * FB)],
            in_specs=[SMEM] + [HBM] * 5 + [VMEM] * 2,
            out_specs=[VMEM, VMEM, HBM],
            scratch_shapes=density_scratch(1)
            + [pltpu.VMEM((FB, COLS * FB), jnp.float32), pltpu.SemaphoreType.DMA((BLK_DEV,))],
            compiler_params=params,
            cost_estimate=pl.CostEstimate(flops=8 * 10**9, bytes_accessed=2 * 10**7, transcendentals=0),
        )(bricks, *tables, density_rows, for_mate, charge)
        mate_pack = with_mate(pack)
        mate_far_part = with_mate(far_part)
        own, mate, charges = pl.pallas_call(
            add_kernel,
            out_shape=[f32(1, CELLS + LAYER), f32(1, CELLS), f32(devices, 1, FB)],
            in_specs=[VMEM] * 5,
            out_specs=[VMEM] * 3,
            compiler_params=pltpu.CompilerParams(vmem_limit_bytes=8 * 2**20),
        )(pack, mate_pack, far_part, mate_far_part, total)
        far = with_far(own)
        charges = lax.all_to_all(charges, "dev", 0, 0, tiled=True)
        mate_far = with_mate(far)
        return pl.pallas_call(
            lambda *refs: ham_kernel(devices, *refs),
            out_shape=[f32(1, CELLS), f32(BLK_DEV * FB, COLS * FB)],
            in_specs=[SMEM] + [HBM] * 4 + [VMEM] * 5 + [HBM],
            out_specs=[VMEM, HBM],
            scratch_shapes=shared_scratch
            + [
                pltpu.VMEM((3, 8, CELLS), jnp.float32),
                pltpu.VMEM((2 * PAIR, WIDE), jnp.float32),
                pltpu.VMEM((BLK_DEV * FB, COLS * FB), jnp.float32),
                pltpu.SemaphoreType.DMA(()),
                pltpu.SemaphoreType.DMA((3, 2)),
                pltpu.SemaphoreType.DMA(()),
            ],
            input_output_aliases={10: 1},
            compiler_params=params,
        )(bricks, *tables, own, mate, far, mate_far, charges, zeroed)

    return jax.shard_map(
        local,
        mesh=mesh,
        in_specs=(P("dev", None), P(), P(), P(), P(), P()),
        out_specs=(P("dev", None), P("dev", None)),
        check_vma=False,
    )
```

```python
import math

import jax
import jax.numpy as jnp
from jax import lax
from jax.experimental import pallas as pl
from jax.experimental.pallas import tpu as pltpu
from jax.sharding import PartitionSpec as P

FB = 128
KB = 8
BLK_DEV = 6
SIDE = 16
LAYER = SIDE * SIDE
CELLS = SIDE * LAYER
WIDE = KB * FB
CHUNK = 1024
SUB = 256
PAIR = 2 * FB
TILE = 8
TILES = 5
COLS = 5 * BLK_DEV

omega = 2.0 / 3.0
four_pi = 4.0 * math.pi
slater = (3.0 / math.pi) ** (1.0 / 3.0)

VMEM = pl.BlockSpec(memory_space=pltpu.VMEM)
SMEM = pl.BlockSpec(memory_space=pltpu.SMEM)
HBM = pl.BlockSpec(memory_space=pltpu.HBM)
LIMIT = 536 * 2**20 // 10


def aligned(index, unit):
    if isinstance(index, int):
        return pl.ds(index * unit, unit)
    return pl.ds(pl.multiple_of(index * unit, unit), unit)


def wrap(value, count):
    return lax.rem(value + 2 * count, count)


def list_blocks(devices, sides, bricks_ref, lists_ref, count_ref):
    own = lax.axis_index("dev")
    for side in sides:
        brick = wrap(own + side - 1, devices)
        ids = [bricks_ref[k, brick] for k in range(KB)]
        owners = [i // BLK_DEV for i in ids]
        held = [(owner == own).astype(jnp.int32) for owner in owners]
        first, second = jnp.int32(0), sum(held)
        count_ref[side] = second
        for i, owner, h in zip(ids, owners, held):
            at = side * KB + jnp.where(h == 1, first, second)
            row = i - owner * BLK_DEV
            lists_ref[0, at] = i
            lists_ref[1, at] = row
            lists_ref[2, at] = wrap(owner - own + 2, devices) * BLK_DEV + row
            lists_ref[3, at] = owner
            first, second = first + h, second + 1 - h


def first_tile(devices):
    own = lax.axis_index("dev")
    return wrap((own - 2) * BLK_DEV, devices * BLK_DEV) // TILE


def fetch_tables(devices, table_refs, tables_ref, sem):
    base = first_tile(devices)
    for t, table_ref in enumerate(table_refs):
        for k in range(TILES):
            tile = lax.rem(base + k, devices * BLK_DEV // TILE)
            pltpu.make_async_copy(
                table_ref.at[aligned(tile, TILE), :], tables_ref.at[t, pl.ds(k * TILE, TILE), :], sem
            ).start()


def factors(devices, side, lists_ref, tables_ref, x_ref, y_ref, z_ref):
    own = lax.axis_index("dev")
    brick = wrap(own + side - 1, devices)
    base = first_tile(devices) * TILE
    points = (lax.broadcasted_iota(jnp.int32, (SIDE, FB), 0).astype(jnp.float32) + 0.5) / SIDE
    for k in range(KB):
        block, owner = lists_ref[0, side * KB + k], lists_ref[3, side * KB + k]
        offset = (wrap(brick - owner + 1, devices) - 1).astype(jnp.float32)
        row = pl.ds(wrap(block - base, devices * BLK_DEV), 1)
        decay = -tables_ref[3, row, :]
        lanes = pl.ds(k * FB, FB)
        along_x = (offset + points) - tables_ref[0, row, :]
        x_ref[:, lanes] = jnp.exp(decay * along_x * along_x)
        for t, out_ref in ((1, y_ref), (2, z_ref)):
            away = points - tables_ref[t, row, :] + 0.5
            away = away - jnp.floor(away) - 0.5
            out_ref[:, lanes] = jnp.exp(decay * away * away)


def orbital_chunk(part, step, x_ref, y_ref, z_ref, orb_ref):
    layers = CHUNK // LAYER
    for k in range(KB):
        lanes = slice(k * FB, (k + 1) * FB)
        x = x_ref[aligned(step, 8), lanes]
        y, z = y_ref[:, lanes], z_ref[:, lanes]
        for i in range(layers):
            xy = x[part * layers + i : part * layers + i + 1] * y
            for j in range(SIDE):
                at = (i * SIDE + j) * SIDE
                orb_ref[at : at + SIDE, lanes] = (xy[j : j + 1] * z).astype(jnp.bfloat16)


def density_of(
    devices, sides, bricks_ref, table_refs, rows_ref,
    lists_ref, count_ref, tables_ref, x_ref, y_ref, z_ref, orb_a, orb_b, dens_ref, res_ref, table_sem, dens_sems,
):
    first, stride = sides
    fetch_tables(devices, table_refs, tables_ref, table_sem)
    slots = dens_ref.shape[0]
    list_blocks(devices, [first + stride * slot for slot in range(slots)], bricks_ref, lists_ref, count_ref)

    def fetch_brick(slot, carry):
        side = first + stride * slot

        def fetch(half, inner):
            for a in range(2):
                row = lists_ref[1, side * KB + half * 2 + a]
                for c in range(KB):
                    pltpu.make_async_copy(
                        rows_ref.at[aligned(row, FB), aligned(lists_ref[2, side * KB + c], FB)],
                        dens_ref.at[slot, aligned(half * 2 + a, FB), pl.ds(c * FB, FB)],
                        dens_sems.at[slot, half],
                    ).start()
            return inner

        return lax.fori_loop(0, count_ref[side] // 2, fetch, carry)

    lax.fori_loop(0, slots, fetch_brick, 0)
    pltpu.make_async_copy(tables_ref, tables_ref, table_sem).wait()

    def one_brick(slot, carry):
        side = first + stride * slot
        factors(devices, side, lists_ref, tables_ref, x_ref, y_ref, z_ref)

        def await_half(half, inner):
            pltpu.make_async_copy(
                rows_ref.at[pl.ds(0, PAIR), pl.ds(0, WIDE)],
                dens_ref.at[slot, aligned(half, PAIR), :],
                dens_sems.at[slot, half],
            ).wait()
            return inner

        lax.fori_loop(0, count_ref[side] // 2, await_half, 0)

        def steps(rows):
            def step(t):
                for part, orb_ref in ((0, orb_a), (1, orb_b)):
                    orbital_chunk(part, t, x_ref, y_ref, z_ref, orb_ref)
                    for s in range(0, CHUNK, SUB):
                        applied = lax.dot_general(
                            orb_ref[s : s + SUB, :], dens_ref[slot, :rows, :], (((1,), (1,)), ((), ())),
                            preferred_element_type=jnp.float32,
                        )
                        product = applied * orb_ref[s : s + SUB, :rows].astype(jnp.float32)
                        total = product[:, :FB]
                        for k in range(FB, rows, FB):
                            total = total + product[:, k : k + FB]
                        at = pl.ds(t * 2 * CHUNK + part * CHUNK + s, SUB)
                        res_ref[slot, :, at] = jnp.sum(total.T, axis=0, keepdims=True)

            for t in range(CELLS // (2 * CHUNK)):
                step(t)

        pl.when(count_ref[side] == 2)(lambda: steps(PAIR))
        pl.when(count_ref[side] != 2)(lambda: steps(2 * PAIR))
        return carry

    lax.fori_loop(0, slots, one_brick, 0)


def folded(row):
    total = row[:, :FB]
    for k in range(1, CELLS // FB):
        total = total + row[:, k * FB : (k + 1) * FB]
    return total


def odd_device():
    return lax.rem(lax.axis_index("dev"), 2)


def beside_kernel(devices, bricks_ref, cx_ref, cy_ref, cz_ref, ex_ref, rows_ref, mate_ref, far_ref, charge_ref, *scratch):
    density_of(devices, (0, 2), bricks_ref, (cx_ref, cy_ref, cz_ref, ex_ref), rows_ref, *scratch)
    res_ref = scratch[9]
    odd = odd_device()
    mate_ref[...] = res_ref[1 - odd]
    far_ref[...] = res_ref[odd]
    charge_ref[...] = folded(res_ref[0] + res_ref[1])


def own_kernel(
    devices, bricks_ref, cx_ref, cy_ref, cz_ref, ex_ref, rows_ref, mate_ref, charge_ref,
    pack_ref, total_ref, zero_out_ref, *scratch
):
    zero_ref, zero_sems = scratch[-2:]
    zero_ref[...] = jnp.zeros_like(zero_ref)
    zero_copies = [
        pltpu.make_async_copy(zero_ref, zero_out_ref.at[pl.ds(r * FB, FB), :], zero_sems.at[r]) for r in range(BLK_DEV)
    ]
    for copy in zero_copies:
        copy.start()
    density_of(devices, (1, 0), bricks_ref, (cx_ref, cy_ref, cz_ref, ex_ref), rows_ref, *scratch[:-2])
    res_ref = scratch[9]
    pack_ref[:, :CELLS] = mate_ref[...]
    pack_ref[:, CELLS:] = res_ref[0]
    total_ref[...] = charge_ref[...] + folded(res_ref[0])
    for copy in zero_copies:
        copy.wait()


def add_kernel(pack_ref, mate_pack_ref, far_ref, mate_far_ref, total_ref, own_ref, mate_ref, charges_ref):
    own = pack_ref[:, CELLS:] + mate_pack_ref[:, :CELLS] + far_ref[...]
    mate = pack_ref[:, :CELLS] + mate_pack_ref[:, CELLS:] + mate_far_ref[...]
    own_ref[:, :CELLS] = own
    own_ref[:, CELLS:] = jnp.where(odd_device() == 1, mate[:, CELLS - LAYER :], mate[:, :LAYER])
    mate_ref[...] = mate
    charges_ref[...] = jnp.broadcast_to(total_ref[...][None], charges_ref.shape)


def potential_of(density, before, after, average):
    lane = lax.broadcasted_iota(jnp.int32, density.shape, 1)
    along_z = lane & (SIDE - 1)
    along_y = (lane // SIDE) & (SIDE - 1)
    scale = omega * four_pi / 6.0
    source = density - average
    one = scale * source
    padded = jnp.concatenate([scale * (before - average), one, scale * (after - average)], axis=1)
    beside = padded[:, :CELLS] + padded[:, 2 * LAYER :]

    def moved(steps):
        return pltpu.roll(one, steps % CELLS, 1)

    beside += jnp.where(along_y > 0, moved(SIDE), moved(SIDE - LAYER))
    beside += jnp.where(along_y < SIDE - 1, moved(-SIDE), moved(LAYER - SIDE))
    beside += jnp.where(along_z > 0, moved(1), moved(1 - SIDE))
    beside += jnp.where(along_z < SIDE - 1, moved(-1), moved(SIDE - 1))
    two = one + omega * ((four_pi * source + beside) / 6.0 - one)
    root = jnp.exp(jnp.log(jnp.abs(density)) * (1.0 / 3.0))
    return two - slater * jnp.where(density < 0.0, -root, root)


def ham_kernel(
    devices, bricks_ref, cx_ref, cy_ref, cz_ref, ex_ref,
    own_ref, mate_ref, far_ref, mate_far_ref, charges_ref, zeroed_ref,
    pot_ref, ham_ref,
    lists_ref, count_ref, tables_ref, x_ref, y_ref, z_ref, orb_a, orb_b, v_ref, acc_ref, sum_ref,
    table_sem, ham_sems, clear_sem,
):
    fetch_tables(devices, (cx_ref, cy_ref, cz_ref, ex_ref), tables_ref, table_sem)
    clearing = pltpu.make_async_copy(ham_ref, sum_ref, clear_sem)
    clearing.start()
    list_blocks(devices, range(3), bricks_ref, lists_ref, count_ref)

    def wide(row):
        return jnp.broadcast_to(row, (8, row.shape[1]))

    odd = odd_device() == 1
    mate, far = mate_ref[...], far_ref[:, :CELLS]
    far_edge, mate_edge = far_ref[:, CELLS:], jnp.where(odd, mate_far_ref[:, CELLS - LAYER : CELLS], mate_far_ref[:, :LAYER])
    mid = wide(own_ref[:, :CELLS])
    left, right = wide(jnp.where(odd, mate, far)), wide(jnp.where(odd, far, mate))
    before, after = wide(jnp.where(odd, mate_edge, far_edge)), wide(jnp.where(odd, far_edge, mate_edge))
    average = jnp.sum(jnp.sum(charges_ref[...], axis=0)) / (devices * CELLS)
    scale = 64.0 / CELLS
    v_ref[0] = scale * potential_of(left, before, mid[:, :LAYER], average)
    own_potential = potential_of(mid, left[:, CELLS - LAYER :], right[:, :LAYER], average)
    v_ref[1] = scale * own_potential
    v_ref[2] = scale * potential_of(right, mid[:, CELLS - LAYER :], after, average)
    pot_ref[...] = own_potential[:1]
    pltpu.make_async_copy(tables_ref, tables_ref, table_sem).wait()

    def await_rows(side, rows_half):
        pltpu.make_async_copy(
            sum_ref.at[pl.ds(0, PAIR), pl.ds(0, WIDE)], ham_ref.at[pl.ds(0, PAIR), pl.ds(0, WIDE)],
            ham_sems.at[side, rows_half],
        ).wait()

    def await_brick(side):
        lax.fori_loop(0, count_ref[side] // 2, lambda half, inner: (await_rows(side, half), inner)[1], 0)

    def one_brick(side, carry):
        factors(devices, side, lists_ref, tables_ref, x_ref, y_ref, z_ref)

        def steps(rows):
            def step(t):
                for part, orb_ref in ((0, orb_a), (1, orb_b)):
                    orbital_chunk(part, t, x_ref, y_ref, z_ref, orb_ref)
                    at = pl.ds(t * 2 * CHUNK + part * CHUNK, CHUNK)
                    v = v_ref[side, pl.ds(0, 1), at]
                    mine = orb_ref[:, :rows].T
                    weighted = (mine.astype(jnp.float32) * v).astype(jnp.bfloat16)
                    for r in range(0, rows, PAIR):
                        product = jnp.dot(weighted[r : r + PAIR], orb_ref[:, r:], preferred_element_type=jnp.float32)
                        if t + part > 0:
                            product += acc_ref[r : r + PAIR, r:]
                        acc_ref[r : r + PAIR, r:] = product

            for t in range(CELLS // (2 * CHUNK)):
                step(t)
            if rows > PAIR:
                acc_ref[PAIR:rows, :PAIR] = acc_ref[:PAIR, PAIR:rows].T
            pl.when(side == 0)(clearing.wait)
            pl.when(side > 0)(lambda: await_brick(jnp.maximum(side - 1, 0)))
            for a in range(rows // FB):
                row = lists_ref[1, side * KB + a]
                for c in range(KB):
                    block = (aligned(row, FB), aligned(lists_ref[2, side * KB + c], FB))
                    sum_ref[block] += acc_ref[a * FB : (a + 1) * FB, c * FB : (c + 1) * FB]
                    pltpu.make_async_copy(sum_ref.at[block], ham_ref.at[block], ham_sems.at[side, a // 2]).start()

        pl.when(count_ref[side] == 2)(lambda: steps(PAIR))
        pl.when(count_ref[side] != 2)(lambda: steps(2 * PAIR))
        return carry

    lax.fori_loop(0, 3, one_brick, 0)
    await_brick(2)


def f32(*shape):
    return jax.ShapeDtypeStruct(shape, jnp.float32)


def solution(mesh):
    devices = mesh.shape["dev"]

    def with_mate(value):
        return lax.ppermute(value, "dev", [(i, i ^ 1) for i in range(devices)])

    def with_far(value):
        return lax.ppermute(value, "dev", [(i, (i + (i % 2) * 2 - 1) % devices) for i in range(devices)])

    shared_scratch = [
        pltpu.SMEM((4, 3 * KB), jnp.int32),
        pltpu.SMEM((3,), jnp.int32),
        pltpu.VMEM((4, TILES * TILE, FB), jnp.float32),
        pltpu.VMEM((SIDE, WIDE), jnp.float32),
        pltpu.VMEM((SIDE, WIDE), jnp.float32),
        pltpu.VMEM((SIDE, WIDE), jnp.float32),
        pltpu.VMEM((CHUNK, WIDE), jnp.bfloat16),
        pltpu.VMEM((CHUNK, WIDE), jnp.bfloat16),
    ]

    def local(density_rows, center_x, center_y, center_z, exponent, brick_blocks):
        tables = [t.reshape(-1, FB) for t in (center_x, center_y, center_z, exponent)]
        bricks = brick_blocks.T
        params = pltpu.CompilerParams(vmem_limit_bytes=LIMIT)

        def density_scratch(slots):
            return shared_scratch + [
                pltpu.VMEM((slots, 2 * PAIR, WIDE), jnp.bfloat16),
                pltpu.VMEM((slots, 1, CELLS), jnp.float32),
                pltpu.SemaphoreType.DMA(()),
                pltpu.SemaphoreType.DMA((slots, 2)),
            ]

        for_mate, for_far, charge = pl.pallas_call(
            lambda *refs: beside_kernel(devices, *refs),
            out_shape=[f32(1, CELLS), f32(1, CELLS), f32(1, FB)],
            in_specs=[SMEM] + [HBM] * 5,
            out_specs=[VMEM] * 3,
            scratch_shapes=density_scratch(2),
            compiler_params=params,
        )(bricks, *tables, density_rows)
        far_part = with_far(for_far)
        pack, total, zeroed = pl.pallas_call(
            lambda *refs: own_kernel(devices, *refs),
            out_shape=[f32(1, 2 * CELLS), f32(1, FB), f32(BLK_DEV * FB, COLS * FB)],
            in_specs=[SMEM] + [HBM] * 5 + [VMEM] * 2,
            out_specs=[VMEM, VMEM, HBM],
            scratch_shapes=density_scratch(1)
            + [pltpu.VMEM((FB, COLS * FB), jnp.float32), pltpu.SemaphoreType.DMA((BLK_DEV,))],
            compiler_params=params,
            cost_estimate=pl.CostEstimate(flops=8 * 10**9, bytes_accessed=2 * 10**7, transcendentals=0),
        )(bricks, *tables, density_rows, for_mate, charge)
        mate_pack = with_mate(pack)
        mate_far_part = with_mate(far_part)
        own, mate, charges = pl.pallas_call(
            add_kernel,
            out_shape=[f32(1, CELLS + LAYER), f32(1, CELLS), f32(devices, 1, FB)],
            in_specs=[VMEM] * 5,
            out_specs=[VMEM] * 3,
            compiler_params=pltpu.CompilerParams(vmem_limit_bytes=8 * 2**20),
        )(pack, mate_pack, far_part, mate_far_part, total)
        far = with_far(own)
        charges = lax.all_to_all(charges, "dev", 0, 0, tiled=True)
        mate_far = with_mate(far)
        return pl.pallas_call(
            lambda *refs: ham_kernel(devices, *refs),
            out_shape=[f32(1, CELLS), f32(BLK_DEV * FB, COLS * FB)],
            in_specs=[SMEM] + [HBM] * 4 + [VMEM] * 5 + [HBM],
            out_specs=[VMEM, HBM],
            scratch_shapes=shared_scratch
            + [
                pltpu.VMEM((3, 8, CELLS), jnp.float32),
                pltpu.VMEM((2 * PAIR, WIDE), jnp.float32),
                pltpu.VMEM((BLK_DEV * FB, COLS * FB), jnp.float32),
                pltpu.SemaphoreType.DMA(()),
                pltpu.SemaphoreType.DMA((3, 2)),
                pltpu.SemaphoreType.DMA(()),
            ],
            input_output_aliases={10: 1},
            compiler_params=params,
        )(bricks, *tables, own, mate, far, mate_far, charges, zeroed)

    return jax.shard_map(
        local,
        mesh=mesh,
        in_specs=(P("dev", None), P(), P(), P(), P(), P()),
        out_specs=(P("dev", None), P("dev", None)),
        check_vma=False,
    )
```
